768 devices in a mesh: rows: 32 (over x, y_hi, core), rep: 24 (over z, y_lo).
Axes of the slice: x: 4, y: 8 (y_hi: 4, y_lo: 2; y = y_hi * 2 + y_lo), z: 12, core: 2. Of those that a mesh axis runs over, the one named last changes fastest.
Arguments:
- features: bfloat16 [24576, 128], P('rows'), may hold values from -6 to 6
- self_weight: bfloat16 [128, 256], replicated, may hold values from -0.5 to 0.5
- neigh_weight: bfloat16 [128, 256], replicated, may hold values from -3 to 3
- bias: float32 [256], replicated, may hold values from -3 to 3
- degree: int32 [24576], P(('rows', 'rep')), may hold values from 16 to 96
- cotangent: bfloat16 [24576, 256], P(('rows', 'rep')), may hold values from -6 to 6
- owners: int32 [24, 4], P('rep'), may hold values from 0 to 31, as said below
- tile_rows: int32 [32, 24, 4, 16], P('rows', 'rep'), may hold values from 0 to 5
- tile_cols: int32 [32, 24, 4, 16], P('rows', 'rep'), may hold values from 0 to 5
- tile_count: int32 [32, 24, 4], P('rows', 'rep'), may hold values from 2 to 16, as said below
- masks: int32 [32, 24, 4, 16, 128, 128], P('rows', 'rep'), may hold values 0 or 1
Outputs:
- hidden: bfloat16 [24576, 256], P(('rows', 'rep'))
- grad_self: float32 [128, 256], replicated
- grad_neigh: float32 [128, 256], replicated
- grad_bias: float32 [256], replicated
The draws below stay inside these ranges and needn't reach their ends.
Inputs may be any that keep to these rules, and one draw needn't show every extreme that they name: Within one index of rep the 4 owners are different row blocks. Slots at and beyond tile_count of a list are empty. Some row blocks hold 16 live tiles in every list of every copy, the others at most 8; at least one row block is of the first kind.
All inputs are finite; a program needn't handle non-finite values. No bound on the sum of `masks` on one device may be relied on, other than what follows from the above.
Results may differ from the reference program's by a relative error of at most 0.014.
Values may be sent and summed in bfloat16 or wider, within the bound.
A program may use at most 32 MiB of HBM per device.

```python
import jax
import jax.numpy as jnp
from jax import lax

F_IN = 128
F = 256
TILE = 128
ROW_TILES = 6
SECTIONS = 4
SLOTS = 16
ROWS_DEV = 768
NODES = 24576
N_ROWS = 32
N_REP = 24


def lead_with(perm, value):
    positions = jnp.arange(perm.shape[0])
    return jnp.where(perm == value, perm[0], jnp.where(positions == 0, value, perm))


def draw_owners(key, part):
    key = jax.random.fold_in(key, 11)
    keys = jax.random.split(key, N_REP)
    perms = jax.vmap(lambda one_key: jax.random.permutation(one_key, N_ROWS))(keys).astype(jnp.int32)
    perms = perms.at[0].set(lead_with(perms[0], N_ROWS - 1))
    perms = perms.at[N_REP - 1].set(lead_with(perms[N_REP - 1], 0))
    return perms[:, :SECTIONS].astype(jnp.int32)


def draw_tile_count(key, part):
    key = jax.random.fold_in(key, 23)
    light_key, heavy_key, pick_key = jax.random.split(key, 3)
    light = jax.random.randint(light_key, (N_ROWS, N_REP, SECTIONS), 2, SLOTS // 2 + 1)
    heavy = jax.random.randint(heavy_key, (N_ROWS,), 0, 4) == 0
    chosen = jax.random.randint(pick_key, (), 0, N_ROWS)
    heavy = heavy | (jnp.arange(N_ROWS) == chosen)
    return jnp.where(heavy[:, None, None], SLOTS, light).astype(jnp.int32)


def plant(array, own_key, low, high):
    shape = array.shape
    spot = [jax.random.randint(jax.random.fold_in(own_key, axis), (), 0, shape[axis]) for axis in range(len(shape))]
    array = array.at[tuple(spot)].set(low)
    longest = shape.index(max(shape))
    spot[longest] = (spot[longest] + 1) % shape[longest]
    return array.at[tuple(spot)].set(high)


def block_scale(own_key, dims, cuts, smallest, largest):
    factor_of = 1.0
    for dim, shards_of in cuts:
        draws = jax.random.uniform(jax.random.fold_in(jax.random.fold_in(own_key, 6), dim), (shards_of,), jnp.float32, smallest / len(cuts), largest / len(cuts))
        factor_of = factor_of * jnp.repeat(jnp.exp(draws), dims[dim] // shards_of).reshape((-1,) + (1,) * (len(dims) - 1 - dim))
    return factor_of


def gaussian(stream_key, dims, width, bound, cuts=(), dtype=jnp.bfloat16):
    entries = width * jax.random.normal(stream_key, dims, jnp.float32)
    if cuts:
        entries = entries * block_scale(stream_key, dims, cuts, -0.22, 0.18)
    return jnp.clip(entries, -bound, bound).astype(dtype)


def setup_inputs(seed: int = 0) -> dict:
    key_of = jax.random.split(jax.random.key(seed), 12)
    features = gaussian(key_of[0], (NODES, F_IN), 1.0, 6.0, ((0, 32),))
    self_weight = gaussian(key_of[1], (F_IN, F), F_IN ** -0.5, 0.5)
    neigh_weight = gaussian(key_of[2], (F_IN, F), (F_IN // 32) ** -0.5, 3.0)
    bias = gaussian(key_of[3], (F,), 0.5, 3.0, (), jnp.float32)
    degree = plant(jax.random.randint(key_of[4], (NODES,), 16, 97), jax.random.fold_in(key_of[4], 1), 16, 96).astype(jnp.int32)
    cotangent = gaussian(key_of[5], (NODES, F), 1.0, 6.0, ((0, 768),))
    owners = draw_owners(jax.random.fold_in(key_of[11], 71), 0)
    tile_rows = plant(jax.random.randint(key_of[7], (N_ROWS, N_REP, SECTIONS, SLOTS), 0, ROW_TILES), jax.random.fold_in(key_of[7], 1), 0, ROW_TILES - 1).astype(jnp.int32)
    tile_cols = plant(jax.random.randint(key_of[8], (N_ROWS, N_REP, SECTIONS, SLOTS), 0, ROW_TILES), jax.random.fold_in(key_of[8], 1), 0, ROW_TILES - 1).astype(jnp.int32)
    tile_count = draw_tile_count(jax.random.fold_in(key_of[11], 71), 0)
    masks = plant((jax.random.randint(key_of[10], (N_ROWS, N_REP, SECTIONS, SLOTS, TILE, TILE), 0, TILE) < 1).astype(jnp.int32), jax.random.fold_in(key_of[10], 1), 0, 1)
    return {"features": features, "self_weight": self_weight, "neigh_weight": neigh_weight, "bias": bias, "degree": degree, "cotangent": cotangent, "owners": owners, "tile_rows": tile_rows, "tile_cols": tile_cols, "tile_count": tile_count, "masks": masks}


def reference(features, self_weight, neigh_weight, bias, degree, cotangent, owners, tile_rows, tile_cols, tile_count, masks):
    tiles = features.reshape(N_ROWS, ROW_TILES, TILE, F_IN)
    tile_grid = jnp.arange(ROW_TILES).astype(jnp.int32)
    slot_ids = jnp.arange(SLOTS).astype(jnp.int32)

    def per_block(index):
        columns = tile_cols[index]
        pieces = tiles[owners[:, :, None], columns].astype(jnp.float32)
        pattern = masks[index].astype(jnp.float32)
        products = jnp.einsum("jskpq,jskqf->jskpf", pattern, pieces, precision=lax.Precision.HIGHEST)
        live_slot = slot_ids[None, None, :] < tile_count[index][:, :, None]
        placing = ((tile_rows[index][..., None] == tile_grid) & live_slot[..., None]).astype(jnp.float32)
        summed = jnp.einsum("jskr,jskpf->rpf", placing, products, precision=lax.Precision.HIGHEST)
        return summed.reshape(ROWS_DEV, F_IN)

    neigh_sum = lax.map(per_block, jnp.arange(N_ROWS).astype(jnp.int32)).reshape(NODES, F_IN)
    neigh_mean = (neigh_sum / degree.astype(jnp.float32)[:, None]).astype(jnp.bfloat16)
    pre = jnp.dot(features, self_weight, preferred_element_type=jnp.float32)
    pre = pre + jnp.dot(neigh_mean, neigh_weight, preferred_element_type=jnp.float32) + bias
    negative = jnp.minimum(pre, 0.0)
    hidden = jnp.where(pre > 0, pre, jnp.expm1(negative)).astype(jnp.bfloat16)
    slope = jnp.where(pre > 0, 1.0, jnp.exp(negative))
    grad_pre = cotangent.astype(jnp.float32) * slope
    grad_low = grad_pre.astype(jnp.bfloat16)
    norm_scale = NODES ** -0.5
    grad_self = jnp.dot(features.T, grad_low, preferred_element_type=jnp.float32) * norm_scale
    grad_neigh = jnp.dot(neigh_mean.T, grad_low, preferred_element_type=jnp.float32) * norm_scale
    grad_bias = jnp.sum(grad_pre, axis=0) * norm_scale
    return hidden, grad_self, grad_neigh, grad_bias
```

```python
import functools

import jax
import jax.numpy as jnp
from jax import lax
from jax.experimental import pallas as pl
from jax.experimental.pallas import tpu as pltpu
from jax.sharding import PartitionSpec as P

MESH = pl.DeviceIdType.MESH
NX, NYH, NC, NZ, NYL = 4, 4, 2, 12, 2
NY = NYH * NYL
TILE = 128
RT = 6
SECTIONS = 4
SLOTS = 16
ROWS = 768
CHIPS = NX * NYH
PIECE = ROWS // CHIPS
SHARE = ROWS // (NZ * NYL)
F_IN = 128
F = 256
NODES = 24576
GROUP = NX * NC
F32 = jnp.float32
BF16 = jnp.bfloat16


def kernel(
    feat, w_self, w_neigh, bias, degree, cot, owners, trow, tcol, tcnt, masks,
    hidden, g_self, g_neigh, g_bias,
    mask_raw, mask_low, got1, give_core, got_core, feats, tiles, prods, acc, y_out, y_in,
    z_out, z_in, pre_own, m1, r1, m2, r2, m3, r3, m4, r4, m5, r5,
    mask_sem, s_send, s1_recv, core_recv, yrecv, xrecv, relay_recv, half_send, half_recv,
    yl_send, yl_recv, z_send, z_recv, g_send, g_recv,
):
    row, rep = lax.axis_index("rows"), lax.axis_index("rep")
    core = lax.rem(row, NC)
    chip = lax.div(row, NC)
    yh = lax.rem(chip, NYH)
    x = lax.div(chip, NYH)
    yl = lax.rem(rep, NYL)
    z = lax.div(rep, NYL)
    y = yh * NYL + yl
    other = 1 - core

    def dev(x_, yh_, c_, z_, yl_):
        return ((x_ * NYH + yh_) * NC + c_, z_ * NYL + yl_)

    def at_y(y_):
        return dev(x, lax.div(y_, NYL), core, z, lax.rem(y_, NYL))

    def at_group(k):
        return dev(lax.div(k, NC), yh, lax.rem(k, NC), z, yl)

    def send(src, dst, ssem, rsem, device):
        copy = pltpu.make_async_remote_copy(
            src_ref=src, dst_ref=dst, send_sem=ssem, recv_sem=rsem, device_id=device, device_id_type=MESH
        )
        copy.start()

    def arrived(buf, sem):
        pltpu.make_async_copy(buf, buf, sem).wait()

    core_mate = dev(x, yh, other, z, yl)
    yl_mate = dev(x, yh, core, z, 1 - yl)
    row_mates = [
        (lax.rem(x + dx, NX), lax.rem(yh + dy, NYH)) for dx in range(NX) for dy in range(NYH) if dx or dy
    ]
    me_k = x * NC + core

    barrier = pltpu.get_barrier_semaphore()

    def greet(device):
        pl.semaphore_signal(barrier, inc=1, device_id=device, device_id_type=MESH)

    for x_, yh_ in row_mates:
        greet(dev(x_, yh_, core, z, yl))
    for dx in range(NX):
        greet(dev(lax.rem(x + dx, NX), yh, other, z, yl))
    for dy in range(NYH):
        greet(dev(x, lax.rem(yh + dy, NYH), core, z, 1 - yl))
    for dz in range(1, NZ):
        greet(dev(x, yh, core, lax.rem(z + dz, NZ), yl))

    mask_copies = [
        pltpu.make_async_copy(masks.at[s], mask_raw.at[s], mask_sem.at[s]) for s in range(SECTIONS)
    ]
    for copy in mask_copies:
        copy.start()
    got1[chip] = feat[pl.ds(pl.multiple_of(chip * PIECE, 16), PIECE), :]
    pl.semaphore_wait(barrier, len(row_mates) + NX + NYH + NZ - 1)

    for x_, yh_ in row_mates:
        there = x_ * NYH + yh_
        send(
            feat.at[pl.ds(pl.multiple_of(there * PIECE, 16), PIECE), :],
            got1.at[chip], s_send.at[0], s1_recv, dev(x_, yh_, core, z, yl),
        )

    own = feat[pl.ds(pl.multiple_of(rep * SHARE, 16), SHARE), :]
    pre_own[...] = jnp.dot(own, w_self[...], preferred_element_type=F32) + bias[...]
    for s in range(SECTIONS):
        mask_copies[s].wait()

        def lower(k, carry, s=s):
            mask_low[s, k] = mask_raw[s, k].astype(F32).astype(BF16)
            return carry

        lax.fori_loop(0, SLOTS, lower, 0, unroll=2)

    arrived(got1.at[pl.ds(0, CHIPS - 1)], s1_recv)

    def chosen(s):
        owner = owners[0, s]
        piece = jnp.zeros((PIECE, F_IN), F32)
        for b in range(CHIPS):
            gap = owner - (NC * b + core)
            piece = piece + got1[b].astype(F32) * (1 - jnp.minimum(gap * gap, 1)).astype(F32)
        return piece

    for t in range(2):
        give_core[t] = chosen(2 * other + t).astype(BF16)
    send(give_core, got_core, s_send.at[1], core_recv, core_mate)
    arrived(got_core, core_recv)
    place = pl.ds(pl.multiple_of(chip * PIECE, 16), PIECE)
    for t in range(2):
        feats[2 * core + t, place, :] = (chosen(2 * core + t) + got_core[t].astype(F32)).astype(BF16)

    def part(x_, yh_):
        start = pl.multiple_of((x_ * NYH + yh_) * PIECE, 16)
        return feats.at[pl.ds(2 * core, 2), pl.ds(start, PIECE), :]

    def line(x_):
        start = pl.multiple_of(x_ * (NYH * PIECE), 16)
        return feats.at[pl.ds(2 * core, 2), pl.ds(start, NYH * PIECE), :]

    def half_line(t, x_):
        start = pl.multiple_of(x_ * (NYH * PIECE), 16)
        return feats.at[2 * core + t, pl.ds(start, NYH * PIECE), :]

    def half(t, x_, yh_):
        start = pl.multiple_of((x_ * NYH + yh_) * PIECE, 16)
        return feats.at[2 * core + t, pl.ds(start, PIECE), :]

    right, left, far = lax.rem(x + 1, NX), lax.rem(x + 3, NX), lax.rem(x + 2, NX)
    to_right, to_left = dev(right, yh, core, z, yl), dev(left, yh, core, z, yl)
    for dy in (2, 1, 3):
        yh_ = lax.rem(yh + dy, NYH)
        send(part(x, yh), part(x, yh), s_send.at[2], yrecv.at[dy], dev(x, yh_, core, z, yl))
    for dy in (0, 1, 3, 2):
        yh_ = lax.rem(yh + NYH - dy, NYH)
        if dy:
            arrived(part(x, yh_), yrecv.at[dy])
        send(part(x, yh_), part(x, yh_), s_send.at[3], xrecv.at[0, dy], to_right)
        send(part(x, yh_), part(x, yh_), s_send.at[3], xrecv.at[1, dy], to_left)
    send(line(x), line(x), half_send, half_recv.at[0], core_mate)
    for dy in (0, 1, 3, 2):
        yh_ = lax.rem(yh + NYH - dy, NYH)
        arrived(part(left, yh_), xrecv.at[0, dy])
        send(half(0, left, yh_), half(0, left, yh_), s_send.at[4], relay_recv.at[0], to_right)
        arrived(part(right, yh_), xrecv.at[1, dy])
        send(half(1, right, yh_), half(1, right, yh_), s_send.at[4], relay_recv.at[1], to_left)
    send(line(left), line(left), half_send, half_recv.at[1], core_mate)
    send(line(right), line(right), half_send, half_recv.at[2], core_mate)
    arrived(half_line(0, far), relay_recv.at[0])
    arrived(half_line(1, far), relay_recv.at[1])
    send(line(far), line(far), half_send, half_recv.at[3], core_mate)

    def multiply(s, base):
        for c in range(RT):
            tiles[c] = feats[s, TILE * c:TILE * c + TILE, :]

        def one(k, carry):
            prods[base + k] = jnp.dot(
                mask_low[s, k], tiles[tcol[0, 0, s, k]], preferred_element_type=F32
            )
            return carry

        lax.fori_loop(0, SLOTS, one, 0, unroll=2)

    def gather_tile(total, r, s, base):
        for k in range(SLOTS):
            gap = trow[0, 0, s, k] - r
            live = (1 - jnp.minimum(gap * gap, 1)) * jnp.minimum(jnp.maximum(tcnt[0, 0, s] - k, 0), 1)
            total = total + live.astype(F32) * prods[base + k]
        return total

    for t in range(2):
        multiply(2 * core + t, t * SLOTS)

    def first_half(r, carry):
        total = jnp.zeros((TILE, F_IN), F32)
        for t in range(2):
            total = gather_tile(total, r, 2 * core + t, t * SLOTS)
        acc[pl.ds(4 * r, 4)] = total.reshape(4, SHARE, F_IN)
        return carry

    lax.fori_loop(0, RT, first_half, 0)

    far_half = feats.at[pl.ds(2 * other, 2)]
    for n in range(4):
        arrived(far_half.at[:, pl.ds(0, NYH * PIECE), :], half_recv.at[n])
    for t in range(2):
        multiply(2 * other + t, t * SLOTS)

    def second_half(step, carry):
        r = lax.rem(lax.div(z, 2) + 1 + step, RT)
        total = acc[pl.ds(4 * r, 4)].reshape(TILE, F_IN)
        for t in range(2):
            total = gather_tile(total, r, 2 * other + t, t * SLOTS)
        acc[pl.ds(4 * r, 4)] = total.reshape(4, SHARE, F_IN)
        for h in range(2):
            y_out[2 * r + h] = acc[4 * r + 2 * h + 1 - yl].astype(BF16)
        send(y_out.at[pl.ds(2 * r, 2)], y_in.at[pl.ds(2 * r, 2)], yl_send, yl_recv.at[r], yl_mate)
        return carry

    lax.fori_loop(0, RT, second_half, 0)

    def to_z(step, carry):
        r = lax.rem(lax.div(z, 2) + 1 + step, RT)
        arrived(y_in.at[pl.ds(2 * r, 2)], yl_recv.at[r])
        for h in range(2):
            z_ = 2 * r + h
            both = acc[4 * r + 2 * h + yl] + y_in[z_].astype(F32)
            acc[4 * r + 2 * h + yl] = both
            z_out[z_] = both.astype(BF16)

            @pl.when(z_ != z)
            def _():
                send(z_out.at[z_], z_in.at[z], z_send, z_recv, dev(x, yh, core, z_, yl))

        return carry

    lax.fori_loop(0, RT, to_z, 0)
    z_in[z] = jnp.zeros((SHARE, F_IN), BF16)
    lanes = lax.broadcasted_iota(jnp.int32, (SHARE, SHARE), 1)
    subs = lax.broadcasted_iota(jnp.int32, (SHARE, SHARE), 0)
    deg = jnp.sum(jnp.where(lanes == subs, degree[...].astype(F32), 0.0), axis=1, keepdims=True)
    total = acc[2 * z + yl]
    arrived(z_in.at[pl.ds(0, NZ - 1)], z_recv)
    for z_ in range(NZ):
        total = total + z_in[z_].astype(F32)

    mean = (total / deg).astype(BF16)
    pre = pre_own[...] + jnp.dot(mean, w_neigh[...], preferred_element_type=F32)
    fall = jnp.exp(jnp.minimum(pre, 0.0))
    up = pre > 0
    hidden[...] = jnp.where(up, pre, fall - 1.0).astype(BF16)
    grad_pre = cot[...].astype(F32) * jnp.where(up, 1.0, fall)
    grad_low = grad_pre.astype(BF16)
    part_bias = jnp.sum(grad_pre, axis=0, keepdims=True)
    both = jnp.concatenate([own, mean], axis=1)
    part = lax.dot_general(both, grad_low, (((0,), (0,)), ((), ())), preferred_element_type=F32)
    line_ids = lax.broadcasted_iota(jnp.int32, (16, TILE), 0)
    bias_tile = jnp.where(
        line_ids == 0, part_bias[:, :TILE], jnp.where(line_ids == 1, part_bias[:, TILE:], 0.0)
    ).astype(BF16)
    for k in range(GROUP):
        m1[k, 0:32, :] = part[32 * k:32 * k + 32, :TILE].astype(BF16)
        m1[k, 32:64, :] = part[32 * k:32 * k + 32, TILE:].astype(BF16)
        m1[k, 64:80, :] = bias_tile
    for d in range(1, GROUP):
        k = lax.rem(me_k + d, GROUP)
        send(m1.at[k], r1.at[me_k], g_send.at[0], g_recv.at[0], at_group(k))
    r1[me_k] = m1[me_k]
    arrived(r1.at[pl.ds(0, GROUP - 1)], g_recv.at[0])
    level = r1[0].astype(F32)
    for k in range(1, GROUP):
        level = level + r1[k].astype(F32)
    for k in range(NY):
        m2[k] = jnp.concatenate([level[8 * k:8 * k + 8], level[64:72]], axis=0).astype(BF16)
    for d in range(1, NY):
        y_ = lax.rem(y + d, NY)
        send(m2.at[y_], r2.at[y], g_send.at[1], g_recv.at[1], at_y(y_))
    r2[y] = m2[y]
    arrived(r2.at[pl.ds(0, NY - 1)], g_recv.at[1])
    level = r2[0].astype(F32)
    for k in range(1, NY):
        level = level + r2[k].astype(F32)
    m3[...] = level.astype(BF16)
    for d in range(1, NZ):
        z_ = lax.rem(z + d, NZ)
        send(m3, r3.at[z], g_send.at[2], g_recv.at[2], dev(x, yh, core, z_, yl))
    r3[z] = m3[...]
    arrived(r3.at[pl.ds(0, NZ - 1)], g_recv.at[2])
    level = r3[0].astype(F32)
    for k in range(1, NZ):
        level = level + r3[k].astype(F32)
    norm = float(NODES) ** -0.5
    level = level * norm
    m4[...] = level[0:8]
    for d in range(1, NY):
        y_ = lax.rem(y + d, NY)
        send(m4, r4.at[y], g_send.at[3], g_recv.at[3], at_y(y_))
    r4[y] = level[0:8]
    g_bias[:, 0:TILE] = level[8:9]
    g_bias[:, TILE:F] = level[9:10]
    arrived(r4.at[pl.ds(0, NY - 1)], g_recv.at[3])
    m5[...] = r4[...].reshape(64, TILE).astype(BF16)
    for d in range(1, GROUP):
        k = lax.rem(me_k + d, GROUP)
        send(m5, r5.at[me_k], g_send.at[4], g_recv.at[4], at_group(k))
    r5[me_k] = m5[...]

    arrived(got1.at[pl.ds(0, CHIPS - 1)], s_send.at[0])
    arrived(give_core, s_send.at[1])
    arrived(feats.at[0, pl.ds(0, 6 * PIECE), :], s_send.at[2])
    arrived(feats.at[0], s_send.at[3])
    arrived(feats.at[0, pl.ds(0, 8 * PIECE), :], s_send.at[4])
    arrived(feats.at[pl.ds(0, 2)], half_send)
    arrived(y_out, yl_send)
    arrived(z_out.at[pl.ds(0, NZ - 1)], z_send)
    arrived(m1.at[pl.ds(0, GROUP - 1)], g_send.at[0])
    arrived(m2.at[pl.ds(0, NY - 1)], g_send.at[1])
    arrived(r3.at[pl.ds(0, NZ - 1)], g_send.at[2])
    arrived(r4.at[pl.ds(0, NY - 1)], g_send.at[3])
    arrived(r5.at[pl.ds(0, GROUP - 1)], g_send.at[4])

    arrived(r5.at[pl.ds(0, GROUP - 1)], g_recv.at[4])
    for k in range(GROUP):
        target = g_self if k < GROUP // 2 else g_neigh
        first = 32 * (k % (GROUP // 2))
        target[first:first + 32, 0:TILE] = r5[k, 0:32, :].astype(F32)
        target[first:first + 32, TILE:F] = r5[k, 32:64, :].astype(F32)


def body(
    features, self_weight, neigh_weight, bias, degree, cotangent, owners, tile_rows, tile_cols, tile_count, masks
):
    vmem = pl.BlockSpec(memory_space=pltpu.VMEM)
    smem = pl.BlockSpec(memory_space=pltpu.SMEM)
    dma = pltpu.SemaphoreType.DMA
    hidden, g_self, g_neigh, g_bias = pl.pallas_call(
        kernel,
        out_shape=(
            jax.ShapeDtypeStruct((SHARE, F), BF16),
            jax.ShapeDtypeStruct((F_IN, F), F32),
            jax.ShapeDtypeStruct((F_IN, F), F32),
            jax.ShapeDtypeStruct((1, F), F32),
        ),
        in_specs=[vmem] * 6 + [smem] * 4 + [pl.BlockSpec(memory_space=pl.ANY)],
        out_specs=(vmem,) * 4,
        scratch_shapes=[
            pltpu.VMEM((SECTIONS, SLOTS, TILE, TILE), jnp.int32),
            pltpu.VMEM((SECTIONS, SLOTS, TILE, TILE), BF16),
            pltpu.VMEM((CHIPS, PIECE, F_IN), BF16),
            pltpu.VMEM((2, PIECE, F_IN), BF16),
            pltpu.VMEM((2, PIECE, F_IN), BF16),
            pltpu.VMEM((SECTIONS, ROWS, F_IN), BF16),
            pltpu.VMEM((RT, TILE, F_IN), BF16),
            pltpu.VMEM((2 * SLOTS, TILE, F_IN), F32),
            pltpu.VMEM((NZ * NYL, SHARE, F_IN), F32),
            pltpu.VMEM((NZ, SHARE, F_IN), BF16),
            pltpu.VMEM((NZ, SHARE, F_IN), BF16),
            pltpu.VMEM((NZ, SHARE, F_IN), BF16),
            pltpu.VMEM((NZ, SHARE, F_IN), BF16),
            pltpu.VMEM((SHARE, F), F32),
            pltpu.VMEM((GROUP, 80, TILE), BF16),
            pltpu.VMEM((GROUP, 80, TILE), BF16),
            pltpu.VMEM((NY, 16, TILE), BF16),
            pltpu.VMEM((NY, 16, TILE), BF16),
            pltpu.VMEM((16, TILE), BF16),
            pltpu.VMEM((NZ, 16, TILE), BF16),
            pltpu.VMEM((8, TILE), F32),
            pltpu.VMEM((NY, 8, TILE), F32),
            pltpu.VMEM((64, TILE), BF16),
            pltpu.VMEM((GROUP, 64, TILE), BF16),
            dma((SECTIONS,)),
            dma((5,)),
            dma,
            dma,
            dma((NYH,)),
            dma((2, NYH)),
            dma((2,)),
            dma,
            dma((4,)),
            dma,
            dma((RT,)),
            dma,
            dma,
            dma((5,)),
            dma((5,)),
        ],
        compiler_params=pltpu.CompilerParams(
            collective_id=0, has_side_effects=True, vmem_limit_bytes=40 * 1024 * 1024
        ),
    )(
        features, self_weight, neigh_weight, bias.reshape(1, F), degree.reshape(1, SHARE), cotangent,
        owners, tile_rows, tile_cols, tile_count, masks.reshape(SECTIONS, SLOTS, TILE, TILE),
    )
    return hidden, g_self, g_neigh, g_bias.reshape(F)


def solution(mesh):
    return jax.shard_map(
        body,
        mesh=mesh,
        in_specs=(
            P("rows", None),
            P(),
            P(),
            P(),
            P(("rows", "rep")),
            P(("rows", "rep"), None),
            P("rep", None),
            P("rows", "rep", None, None),
            P("rows", "rep", None, None),
            P("rows", "rep", None),
            P("rows", "rep", None, None, None, None),
        ),
        out_specs=(P(("rows", "rep"), None), P(), P(), P()),
        check_vma=False,
    )
```

```python
import functools

import jax
import jax.numpy as jnp
from jax import lax
from jax.experimental import pallas as pl
from jax.experimental.pallas import tpu as pltpu
from jax.sharding import PartitionSpec as P

MESH = pl.DeviceIdType.MESH
NX, NYH, NC, NZ, NYL = 4, 4, 2, 12, 2
NY = NYH * NYL
TILE = 128
RT = 6
SECTIONS = 4
SLOTS = 16
ROWS = 768
CHIPS = NX * NYH
PIECE = ROWS // CHIPS
SHARE = ROWS // (NZ * NYL)
F_IN = 128
F = 256
NODES = 24576
F32 = jnp.float32
BF16 = jnp.bfloat16


def kernel(
    feat_h, w_self_h, w_neigh_h, bias_h, degree_h, cot_h, owners_h, trow_h, tcol_h, tcnt_h, masks,
    hidden, grads, g_bias,
    feat, w_self, w_neigh, bias, degree, cot, owners, trow, tcol, tcnt,
    mask_raw, mask_low, got1, give_core, got_core, feats, tiles, prods, acc, y_out, y_in,
    z_out, z_in, pre_own, pair_out, pair_in, bias_out, bias_in, bias_sum, bias_far,
    m1, r1, m3, r3, m4, r4, r5,
    in_sem, mask_sem, s_send, s1_recv, core_recv, yrecv, xrecv, far_recv, relay_recv, half_send, half_recv,
    yl_send, yl_recv, z_send, z_recv, g_send, g_recv,
):
    row, rep = lax.axis_index("rows"), lax.axis_index("rep")
    core = lax.rem(row, NC)
    chip = lax.div(row, NC)
    yh = lax.rem(chip, NYH)
    x = lax.div(chip, NYH)
    yl = lax.rem(rep, NYL)
    z = lax.div(rep, NYL)
    y = yh * NYL + yl
    other = 1 - core

    def dev(x_, yh_, c_, z_, yl_):
        return ((x_ * NYH + yh_) * NC + c_, z_ * NYL + yl_)

    def at_plane(x_, y_):
        return dev(x_, lax.div(y_, NYL), core, z, lax.rem(y_, NYL))

    def send(src, dst, ssem, rsem, device):
        copy = pltpu.make_async_remote_copy(
            src_ref=src, dst_ref=dst, send_sem=ssem, recv_sem=rsem, device_id=device, device_id_type=MESH
        )
        copy.start()

    def arrived(buf, sem):
        pltpu.make_async_copy(buf, buf, sem).wait()

    core_mate = dev(x, yh, other, z, yl)
    yl_mate = dev(x, yh, core, z, 1 - yl)
    plane = [(lax.rem(x + dx, NX), lax.rem(y + dy, NY)) for dx in (2, 1, 3, 0) for dy in (4, 3, 5, 2, 6, 1, 7, 0)]
    plane = plane[:-1]
    me_q = x * NY + y

    pairs = (
        (feat_h, feat), (owners_h, owners), (w_self_h, w_self), (bias_h, bias), (trow_h, trow), (tcol_h, tcol),
        (tcnt_h, tcnt), (w_neigh_h, w_neigh), (degree_h, degree), (cot_h, cot),
    )
    loads = [pltpu.make_async_copy(a, b, in_sem.at[n]) for n, (a, b) in enumerate(pairs)]
    for copy in loads:
        copy.start()
    barrier = pltpu.get_barrier_semaphore()

    def greet(device):
        pl.semaphore_signal(barrier, inc=1, device_id=device, device_id_type=MESH)

    for dz in (6, 5, 7, 4, 8, 3, 9, 2, 10, 1, 11):
        greet(dev(x, yh, core, lax.rem(z + dz, NZ), yl))
    for x_, y_ in plane:
        greet(at_plane(x_, y_))
    greet(core_mate)

    mask_copies = [
        pltpu.make_async_copy(masks.at[s], mask_raw.at[s], mask_sem.at[s]) for s in range(SECTIONS)
    ]
    for copy in mask_copies:
        copy.start()
    loads[0].wait()
    got1[chip] = feat[pl.ds(pl.multiple_of(chip * PIECE, 16), PIECE), :]
    pl.semaphore_wait(barrier, len(plane) + NZ)

    near, across = lax.rem(yh + 2 * yl + NYH - 1, NYH), lax.rem(yh + 2, NYH)
    shares = [(2, across, 1 - yl), (1, across, 1 - yl), (3, across, 1 - yl), (0, across, 1 - yl)]
    shares += [(dx, near, yl_) for dx in (2, 1, 3, 0) for yl_ in range(NYL)]
    shares += [(dx, yh, yl) for dx in (2, 1, 3)]
    for dx, yh_, yl_ in shares:
        x_ = lax.rem(x + dx, NX)
        there = x_ * NYH + yh_
        send(
            feat.at[pl.ds(pl.multiple_of(there * PIECE, 16), PIECE), :],
            got1.at[chip], s_send.at[0], s1_recv, dev(x_, yh_, core, z, yl_),
        )

    for copy in loads[1:]:
        copy.wait()
    own = feat[pl.ds(pl.multiple_of(rep * SHARE, 16), SHARE), :]
    pre_own[...] = jnp.dot(own, w_self[...], preferred_element_type=F32) + bias[...]
    for s in range(SECTIONS):
        mask_copies[s].wait()

        def lower(k, carry, s=s):
            mask_low[s, k] = mask_raw[s, k].astype(F32).astype(BF16)
            return carry

        lax.fori_loop(0, SLOTS, lower, 0, unroll=2)

    arrived(got1.at[pl.ds(0, CHIPS - 1)], s1_recv)

    def chosen(s):
        owner = owners[0, s]
        piece = jnp.zeros((PIECE, F_IN), F32)
        for b in range(CHIPS):
            gap = owner - (NC * b + core)
            piece = piece + got1[b].astype(F32) * (1 - jnp.minimum(gap * gap, 1)).astype(F32)
        return piece

    for t in range(2):
        give_core[t] = chosen(2 * other + t).astype(BF16)
    send(give_core, got_core, s_send.at[1], core_recv, core_mate)
    arrived(got_core, core_recv)
    place = pl.ds(pl.multiple_of(chip * PIECE, 16), PIECE)
    for t in range(2):
        feats[2 * core + t, place, :] = (chosen(2 * core + t) + got_core[t].astype(F32)).astype(BF16)

    def part(x_, yh_):
        start = pl.multiple_of((x_ * NYH + yh_) * PIECE, 16)
        return feats.at[pl.ds(2 * core, 2), pl.ds(start, PIECE), :]

    def line(x_):
        start = pl.multiple_of(x_ * (NYH * PIECE), 16)
        return feats.at[pl.ds(2 * core, 2), pl.ds(start, NYH * PIECE), :]

    def half(t, x_, yh_):
        start = pl.multiple_of((x_ * NYH + yh_) * PIECE, 16)
        return feats.at[2 * core + t, pl.ds(start, PIECE), :]

    right, left, far = lax.rem(x + 1, NX), lax.rem(x + 3, NX), lax.rem(x + 2, NX)
    to_right, to_left = dev(right, yh, core, z, yl), dev(left, yh, core, z, yl)
    for dy in (2, 1, 3):
        yh_ = lax.rem(yh + dy, NYH)
        send(part(x, yh), part(x, yh), s_send.at[2], yrecv.at[dy], dev(x, yh_, core, z, yl))
    to_far = dev(far, yh, core, z, yl)
    for dy in (0, 1, 3, 2):
        yh_ = lax.rem(yh + NYH - dy, NYH)
        if dy:
            arrived(part(x, yh_), yrecv.at[dy])
        if dy == 2:
            send(part(x, yh_), part(x, yh_), s_send.at[3], far_recv, to_far)
        send(part(x, yh_), part(x, yh_), s_send.at[3], xrecv.at[0, dy], to_right)
        send(part(x, yh_), part(x, yh_), s_send.at[3], xrecv.at[1, dy], to_left)
    send(line(x), line(x), half_send, half_recv.at[0], core_mate)
    for dy in (0, 1, 3, 2):
        yh_ = lax.rem(yh + NYH - dy, NYH)
        arrived(part(left, yh_), xrecv.at[0, dy])
        if dy == 2:
            arrived(part(right, yh_), xrecv.at[1, dy])
            break
        send(half(0, left, yh_), half(0, left, yh_), s_send.at[4], relay_recv.at[0], to_right)
        arrived(part(right, yh_), xrecv.at[1, dy])
        send(half(1, right, yh_), half(1, right, yh_), s_send.at[4], relay_recv.at[1], to_left)
    send(line(left), line(left), half_send, half_recv.at[1], core_mate)
    send(line(right), line(right), half_send, half_recv.at[2], core_mate)
    arrived(feats.at[0, pl.ds(0, 3 * PIECE), :], relay_recv.at[0])
    arrived(feats.at[0, pl.ds(0, 3 * PIECE), :], relay_recv.at[1])
    arrived(part(far, across), far_recv)
    send(line(far), line(far), half_send, half_recv.at[3], core_mate)

    def multiply(s, base):
        for c in range(RT):
            tiles[c] = feats[s, TILE * c:TILE * c + TILE, :]

        def one(k, carry):
            prods[base + k] = jnp.dot(
                mask_low[s, k], tiles[tcol[0, 0, s, k]], preferred_element_type=F32
            )
            return carry

        lax.fori_loop(0, SLOTS, one, 0, unroll=2)

    def gather_tile(total, r, s, base):
        for k in range(SLOTS):
            gap = trow[0, 0, s, k] - r
            live = (1 - jnp.minimum(gap * gap, 1)) * jnp.minimum(jnp.maximum(tcnt[0, 0, s] - k, 0), 1)
            total = total + live.astype(F32) * prods[base + k]
        return total

    for t in range(2):
        multiply(2 * core + t, t * SLOTS)

    def first_half(r, carry):
        total = jnp.zeros((TILE, F_IN), F32)
        for t in range(2):
            total = gather_tile(total, r, 2 * core + t, t * SLOTS)
        acc[pl.ds(4 * r, 4)] = total.reshape(4, SHARE, F_IN)
        return carry

    lax.fori_loop(0, RT, first_half, 0)

    far_half = feats.at[pl.ds(2 * other, 2)]
    for n in range(4):
        arrived(far_half.at[:, pl.ds(0, NYH * PIECE), :], half_recv.at[n])
    for t in range(2):
        multiply(2 * other + t, t * SLOTS)

    def second_half(step, carry):
        r = lax.rem(lax.div(z, 2) + 1 + step, RT)
        total = acc[pl.ds(4 * r, 4)].reshape(TILE, F_IN)
        for t in range(2):
            total = gather_tile(total, r, 2 * other + t, t * SLOTS)
        acc[pl.ds(4 * r, 4)] = total.reshape(4, SHARE, F_IN)
        for h in range(2):
            y_out[2 * r + h] = acc[4 * r + 2 * h + 1 - yl].astype(BF16)
        send(y_out.at[pl.ds(2 * r, 2)], y_in.at[pl.ds(2 * r, 2)], yl_send, yl_recv.at[r], yl_mate)
        return carry

    lax.fori_loop(0, RT, second_half, 0)

    def to_z(step, carry):
        r = lax.rem(lax.div(z, 2) + 1 + step, RT)
        arrived(y_in.at[pl.ds(2 * r, 2)], yl_recv.at[r])
        for h in range(2):
            z_ = 2 * r + h
            both = acc[4 * r + 2 * h + yl] + y_in[z_].astype(F32)
            acc[4 * r + 2 * h + yl] = both
            z_out[z_] = both.astype(BF16)

            @pl.when(z_ != z)
            def _():
                send(z_out.at[z_], z_in.at[z], z_send, z_recv, dev(x, yh, core, z_, yl))

        return carry

    lax.fori_loop(0, RT, to_z, 0)
    z_in[z] = jnp.zeros((SHARE, F_IN), BF16)
    lanes = lax.broadcasted_iota(jnp.int32, (SHARE, SHARE), 1)
    subs = lax.broadcasted_iota(jnp.int32, (SHARE, SHARE), 0)
    deg = jnp.sum(jnp.where(lanes == subs, degree[...].astype(F32), 0.0), axis=1, keepdims=True)
    total = acc[2 * z + yl]
    arrived(z_in.at[pl.ds(0, NZ - 1)], z_recv)
    for z_ in range(NZ):
        total = total + z_in[z_].astype(F32)

    mean = (total / deg).astype(BF16)
    pre = pre_own[...] + jnp.dot(mean, w_neigh[...], preferred_element_type=F32)
    fall = jnp.exp(jnp.minimum(pre, 0.0))
    up = pre > 0
    hidden[...] = jnp.where(up, pre, fall - 1.0).astype(BF16)
    grad_pre = cot[...].astype(F32) * jnp.where(up, 1.0, fall)
    grad_low = grad_pre.astype(BF16)
    part_bias = jnp.sum(grad_pre, axis=0, keepdims=True)
    first_core = core == 0
    pair_out[:, 0:F_IN] = jnp.where(first_core, mean, own)
    pair_out[:, F_IN:] = grad_low
    bias_out[...] = jnp.broadcast_to(
        jnp.where(first_core, part_bias[:, F_IN:], part_bias[:, :F_IN]), (8, F_IN)
    )
    send(pair_out, pair_in, g_send.at[0], g_recv.at[0], core_mate)
    send(bias_out, bias_in, g_send.at[1], g_recv.at[1], core_mate)
    over_nodes = (((0,), (0,)), ((), ()))
    part = lax.dot_general(jnp.where(first_core, own, mean), grad_low, over_nodes, preferred_element_type=F32)
    half_bias = jnp.where(first_core, part_bias[:, :F_IN], part_bias[:, F_IN:])
    arrived(pair_in, g_recv.at[0])
    arrived(bias_in, g_recv.at[1])
    part = part + lax.dot_general(
        pair_in[:, 0:F_IN], pair_in[:, F_IN:], over_nodes, preferred_element_type=F32
    )
    line_ids = lax.broadcasted_iota(jnp.int32, (8, TILE), 0)
    bias_tile = jnp.where(line_ids == 0, half_bias + bias_in[...], 0.0)
    for q in range(NX * NY):
        block = part[8 * (q // 2):8 * (q // 2) + 8, TILE * (q % 2):TILE * (q % 2) + TILE]
        m1[q] = jnp.concatenate([block, bias_tile], axis=0).astype(BF16)
    for x_, y_ in plane:
        send(m1.at[x_ * NY + y_], r1.at[me_q], g_send.at[2], g_recv.at[2], at_plane(x_, y_))
    r1[me_q] = m1[me_q]
    arrived(r1.at[pl.ds(0, NX * NY - 1)], g_recv.at[2])
    level = r1[0].astype(F32)
    for q in range(1, NX * NY):
        level = level + r1[q].astype(F32)
    m3[...] = level.astype(BF16)
    for dz in (6, 5, 7, 4, 8, 3, 9, 2, 10, 1, 11):
        send(m3, r3.at[z], g_send.at[3], g_recv.at[3], dev(x, yh, core, lax.rem(z + dz, NZ), yl))
    r3[z] = m3[...]
    arrived(r3.at[pl.ds(0, NZ - 1)], g_recv.at[3])
    level = r3[0].astype(F32)
    for k in range(1, NZ):
        level = level + r3[k].astype(F32)
    level = level * float(NODES) ** -0.5
    m4[...] = level[0:8]
    for x_, y_ in plane:
        send(m4, r4.at[me_q], g_send.at[4], g_recv.at[4], at_plane(x_, y_))
    r4[me_q] = level[0:8]
    bias_sum[...] = level[8:16]
    send(bias_sum, bias_far, g_send.at[6], g_recv.at[6], core_mate)
    arrived(r4.at[pl.ds(0, NX * NY - 1)], g_recv.at[4])
    send(r4, r5, g_send.at[5], g_recv.at[5], core_mate)
    for q in range(NX * NY):
        grads[core, 8 * (q // 2):8 * (q // 2) + 8, TILE * (q % 2):TILE * (q % 2) + TILE] = r4[q]

    arrived(got1.at[pl.ds(0, CHIPS - 1)], s_send.at[0])
    arrived(give_core, s_send.at[1])
    arrived(feats.at[0, pl.ds(0, 6 * PIECE), :], s_send.at[2])
    arrived(feats.at[pl.ds(0, 3), pl.ds(0, 6 * PIECE), :], s_send.at[3])
    arrived(feats.at[0, pl.ds(0, 6 * PIECE), :], s_send.at[4])
    arrived(feats.at[pl.ds(0, 2)], half_send)
    arrived(y_out, yl_send)
    arrived(z_out.at[pl.ds(0, NZ - 1)], z_send)
    arrived(pair_out, g_send.at[0])
    arrived(bias_out, g_send.at[1])
    arrived(m1.at[pl.ds(0, NX * NY - 1)], g_send.at[2])
    arrived(r3.at[pl.ds(0, NZ - 1)], g_send.at[3])
    arrived(r4.at[pl.ds(0, NX * NY - 1)], g_send.at[4])
    arrived(bias_sum, g_send.at[6])
    arrived(r4, g_send.at[5])

    arrived(bias_far, g_recv.at[6])
    near_bias, far_bias = bias_sum[0:1, :], bias_far[0:1, :]
    g_bias[:, 0:F_IN] = jnp.where(first_core, near_bias, far_bias)
    g_bias[:, F_IN:] = jnp.where(first_core, far_bias, near_bias)
    arrived(r5, g_recv.at[5])
    for q in range(NX * NY):
        grads[other, 8 * (q // 2):8 * (q // 2) + 8, TILE * (q % 2):TILE * (q % 2) + TILE] = r5[q]


def body(
    features, self_weight, neigh_weight, bias, degree, cotangent, owners, tile_rows, tile_cols, tile_count, masks
):
    vmem = pl.BlockSpec(memory_space=pltpu.VMEM)
    dma = pltpu.SemaphoreType.DMA
    hidden, grads, g_bias = pl.pallas_call(
        kernel,
        out_shape=(
            jax.ShapeDtypeStruct((SHARE, F), BF16),
            jax.ShapeDtypeStruct((NC, F_IN, F), F32),
            jax.ShapeDtypeStruct((1, F), F32),
        ),
        in_specs=[pl.BlockSpec(memory_space=pl.ANY)] * 11,
        out_specs=(vmem,) * 3,
        scratch_shapes=[
            pltpu.VMEM((ROWS, F_IN), BF16),
            pltpu.VMEM((F_IN, F), BF16),
            pltpu.VMEM((F_IN, F), BF16),
            pltpu.VMEM((1, F), F32),
            pltpu.VMEM((1, SHARE), jnp.int32),
            pltpu.VMEM((SHARE, F), BF16),
            pltpu.SMEM((1, SECTIONS), jnp.int32),
            pltpu.SMEM((1, 1, SECTIONS, SLOTS), jnp.int32),
            pltpu.SMEM((1, 1, SECTIONS, SLOTS), jnp.int32),
            pltpu.SMEM((1, 1, SECTIONS), jnp.int32),
            pltpu.VMEM((SECTIONS, SLOTS, TILE, TILE), jnp.int32),
            pltpu.VMEM((SECTIONS, SLOTS, TILE, TILE), BF16),
            pltpu.VMEM((CHIPS, PIECE, F_IN), BF16),
            pltpu.VMEM((2, PIECE, F_IN), BF16),
            pltpu.VMEM((2, PIECE, F_IN), BF16),
            pltpu.VMEM((SECTIONS, ROWS, F_IN), BF16),
            pltpu.VMEM((RT, TILE, F_IN), BF16),
            pltpu.VMEM((2 * SLOTS, TILE, F_IN), F32),
            pltpu.VMEM((NZ * NYL, SHARE, F_IN), F32),
            pltpu.VMEM((NZ, SHARE, F_IN), BF16),
            pltpu.VMEM((NZ, SHARE, F_IN), BF16),
            pltpu.VMEM((NZ, SHARE, F_IN), BF16),
            pltpu.VMEM((NZ, SHARE, F_IN), BF16),
            pltpu.VMEM((SHARE, F), F32),
            pltpu.VMEM((SHARE, F_IN + F), BF16),
            pltpu.VMEM((SHARE, F_IN + F), BF16),
            pltpu.VMEM((8, F_IN), F32),
            pltpu.VMEM((8, F_IN), F32),
            pltpu.VMEM((8, F_IN), F32),
            pltpu.VMEM((8, F_IN), F32),
            pltpu.VMEM((NX * NY, 16, TILE), BF16),
            pltpu.VMEM((NX * NY, 16, TILE), BF16),
            pltpu.VMEM((16, TILE), BF16),
            pltpu.VMEM((NZ, 16, TILE), BF16),
            pltpu.VMEM((8, TILE), F32),
            pltpu.VMEM((NX * NY, 8, TILE), F32),
            pltpu.VMEM((NX * NY, 8, TILE), F32),
            dma((10,)),
            dma((SECTIONS,)),
            dma((5,)),
            dma,
            dma,
            dma((NYH,)),
            dma((2, NYH)),
            dma,
            dma((2,)),
            dma,
            dma((4,)),
            dma,
            dma((RT,)),
            dma,
            dma,
            dma((7,)),
            dma((7,)),
        ],
        compiler_params=pltpu.CompilerParams(
            collective_id=0, has_side_effects=True, vmem_limit_bytes=60 * 1024 * 1024
        ),
    )(
        features, self_weight, neigh_weight, bias.reshape(1, F), degree.reshape(1, SHARE), cotangent,
        owners, tile_rows, tile_cols, tile_count, masks.reshape(SECTIONS, SLOTS, TILE, TILE),
    )
    return hidden, grads[0], grads[1], g_bias.reshape(F)


def solution(mesh):
    return jax.shard_map(
        body,
        mesh=mesh,
        in_specs=(
            P("rows", None),
            P(),
            P(),
            P(),
            P(("rows", "rep")),
            P(("rows", "rep"), None),
            P("rep", None),
            P("rows", "rep", None, None),
            P("rows", "rep", None, None),
            P("rows", "rep", None),
            P("rows", "rep", None, None, None, None),
        ),
        out_specs=(P(("rows", "rep"), None), P(), P(), P()),
        check_vma=False,
    )
```

```python
import functools

import jax
import jax.numpy as jnp
from jax import lax
from jax.experimental import pallas as pl
from jax.experimental.pallas import tpu as pltpu
from jax.sharding import PartitionSpec as P

MESH = pl.DeviceIdType.MESH
NX, NYH, NC, NZ, NYL = 4, 4, 2, 12, 2
NY = NYH * NYL
TILE = 128
RT = 6
SECTIONS = 4
SLOTS = 16
ROWS = 768
CHIPS = NX * NYH
PIECE = ROWS // CHIPS
SHARE = ROWS // (NZ * NYL)
OWNERS = NX * NY // 2
F_IN = 128
F = 256
NODES = 24576
F32 = jnp.float32
BF16 = jnp.bfloat16


def kernel(
    feat_h, w_self_h, w_neigh_h, bias_h, degree_h, cot_h, owners_h, trow_h, tcol_h, tcnt_h, masks,
    hidden, grads, g_bias,
    feat, w_self, w_neigh, bias, degree, cot, owners, owners_v, owners_mate_v, owners_mate, trow, tcol, tcnt,
    before, last, mask_raw, mask_low, got1, give_core, got_core, feats, part_mate, tiles, sums, acc, y_out, y_in,
    z_out, z_in, pre_own, pair_out, pair_in, bias_out, bias_in, bias_sum, bias_far,
    m1, r1, m3, r3, m4, r4, r5, bias_tile, rb, m3b, r3b,
    in_sem, mask_sem, o_send, o_recv, o_copy, s_send, s1_recv, core_recv, yrecv, xrecv, far_recv, relay_recv, half_send, half_recv,
    yl_send, yl_recv, z_send, z_recv, g_send, g_recv,
):
    row, rep = lax.axis_index("rows"), lax.axis_index("rep")
    core = lax.rem(row, NC)
    chip = lax.div(row, NC)
    yh = lax.rem(chip, NYH)
    x = lax.div(chip, NYH)
    yl = lax.rem(rep, NYL)
    z = lax.div(rep, NYL)
    y = yh * NYL + yl
    other = 1 - core

    def dev(x_, yh_, c_, z_, yl_):
        return ((x_ * NYH + yh_) * NC + c_, z_ * NYL + yl_)

    def at_plane(x_, y_):
        return dev(x_, lax.div(y_, NYL), core, z, lax.rem(y_, NYL))

    def send(src, dst, ssem, rsem, device):
        copy = pltpu.make_async_remote_copy(
            src_ref=src, dst_ref=dst, send_sem=ssem, recv_sem=rsem, device_id=device, device_id_type=MESH
        )
        copy.start()

    def arrived(buf, sem):
        pltpu.make_async_copy(buf, buf, sem).wait()

    core_mate = dev(x, yh, other, z, yl)
    yl_mate = dev(x, yh, core, z, 1 - yl)
    plane = [(lax.rem(x + dx, NX), lax.rem(y + dy, NY)) for dx in (2, 1, 3, 0) for dy in (4, 3, 5, 2, 6, 1, 7, 0)]
    plane = plane[:-1]
    me_q = x * NY + y

    pairs = (
        (feat_h, feat), (owners_h, owners_v), (owners_h, owners), (w_self_h, w_self), (bias_h, bias), (trow_h, trow), (tcol_h, tcol),
        (tcnt_h, tcnt), (w_neigh_h, w_neigh), (degree_h, degree), (cot_h, cot),
    )
    loads = [pltpu.make_async_copy(a, b, in_sem.at[n]) for n, (a, b) in enumerate(pairs)]
    for copy in loads:
        copy.start()
    barrier = pltpu.get_barrier_semaphore()

    def greet(device):
        pl.semaphore_signal(barrier, inc=1, device_id=device, device_id_type=MESH)

    for dz in (6, 5, 7, 4, 8, 3, 9, 2, 10, 1, 11):
        greet(dev(x, yh, core, lax.rem(z + dz, NZ), yl))
    for x_, y_ in plane:
        greet(at_plane(x_, y_))
    greet(core_mate)

    mask_copies = [
        pltpu.make_async_copy(masks.at[s], mask_raw.at[s], mask_sem.at[s]) for s in range(SECTIONS)
    ]
    for copy in mask_copies:
        copy.start()
    loads[0].wait()
    loads[1].wait()
    loads[2].wait()
    got1[chip] = feat[pl.ds(pl.multiple_of(chip * PIECE, 16), PIECE), :]
    pl.semaphore_wait(barrier, len(plane) + NZ)

    send(owners_v, owners_mate_v, o_send, o_recv, yl_mate)
    near, across = lax.rem(yh + 2 * yl + NYH - 1, NYH), lax.rem(yh + 2, NYH)
    shares = [(2, across, 1 - yl), (1, across, 1 - yl), (3, across, 1 - yl), (0, across, 1 - yl)]
    shares += [(dx, near, yl_) for dx in (2, 1, 3, 0) for yl_ in range(NYL)]
    shares += [(dx, yh, yl) for dx in (2, 1, 3)]
    for dx, yh_, yl_ in shares:
        x_ = lax.rem(x + dx, NX)
        there = x_ * NYH + yh_
        send(
            feat.at[pl.ds(pl.multiple_of(there * PIECE, 16), PIECE), :],
            got1.at[chip], s_send.at[0], s1_recv, dev(x_, yh_, core, z, yl_),
        )

    for copy in loads[3:]:
        copy.wait()
    own = feat[pl.ds(pl.multiple_of(rep * SHARE, 16), SHARE), :]
    pre_own[...] = jnp.dot(own, w_self[...], preferred_element_type=F32) + bias[...]
    for s in range(SECTIONS):
        mask_copies[s].wait()

        def lower(k, carry, s=s):
            mask_low[s, k] = mask_raw[s, k].astype(F32).astype(BF16)
            return carry

        lax.fori_loop(0, SLOTS, lower, 0, unroll=2)

    def chain(t, ends):
        s = lax.rem(2 * core + t, SECTIONS)
        count = tcnt[0, 0, s]
        ends = list(ends)
        for k in range(SLOTS):
            live = jnp.minimum(jnp.maximum(count - k, 0), 1)
            spot = 1 + t * SLOTS + k
            link = 0
            for r in range(RT):
                gap = trow[0, 0, s, k] - r
                same = live * (1 - jnp.minimum(gap * gap, 1))
                link = link + same * ends[r]
                ends[r] = ends[r] + same * (spot - ends[r])
            before[t, k] = link
        return tuple(ends)

    ends = lax.fori_loop(0, SECTIONS, chain, (jnp.int32(0),) * RT)
    for r in range(RT):
        last[r] = ends[r]
    sums[0] = jnp.zeros((TILE, F_IN), F32)
    arrived(owners_mate_v, o_recv)
    fetch = pltpu.make_async_copy(owners_mate_v, owners_mate, o_copy)
    fetch.start()
    fetch.wait()
    arrived(got1.at[pl.ds(0, CHIPS - 1)], s1_recv)

    def chosen(table, s):
        owner = table[0, s]
        piece = jnp.zeros((PIECE, F_IN), F32)
        for b in range(CHIPS):
            gap = owner - (NC * b + core)
            piece = piece + got1[b].astype(F32) * (1 - jnp.minimum(gap * gap, 1)).astype(F32)
        return piece

    for t in range(2):
        give_core[0, t] = chosen(owners, 2 * other + t).astype(BF16)
        give_core[1, t] = chosen(owners_mate, 2 * other + t).astype(BF16)
    send(give_core, got_core, s_send.at[1], core_recv, core_mate)
    mine = [chosen(table, 2 * core + t) for table in (owners, owners_mate) for t in range(2)]
    arrived(got_core, core_recv)
    place = pl.ds(pl.multiple_of(chip * PIECE, 16), PIECE)
    for t in range(2):
        feats[2 * core + t, place, :] = (mine[t] + got_core[0, t].astype(F32)).astype(BF16)
        part_mate[t] = (mine[2 + t] + got_core[1, t].astype(F32)).astype(BF16)

    here = feats.at[pl.ds(2 * core, 2), place, :]

    def line(x_):
        start = pl.multiple_of(x_ * (NYH * PIECE), 16)
        return feats.at[pl.ds(2 * core, 2), pl.ds(start, NYH * PIECE), :]

    def part(x_, yh_):
        start = pl.multiple_of((x_ * NYH + yh_) * PIECE, 16)
        return feats.at[pl.ds(2 * core, 2), pl.ds(start, PIECE), :]

    def half(t, x_, yh_):
        start = pl.multiple_of((x_ * NYH + yh_) * PIECE, 16)
        return feats.at[2 * core + t, pl.ds(start, PIECE), :]

    right, left, far = lax.rem(x + 1, NX), lax.rem(x + 3, NX), lax.rem(x + 2, NX)
    to_right, to_left, to_far = (dev(x_, yh, core, z, yl) for x_ in (right, left, far))
    beside = lax.rem(yh + 1 - 2 * yl + NYH, NYH)
    send(part_mate, here, s_send.at[2], yrecv.at[2], dev(x, across, core, z, 1 - yl))
    send(part_mate, here, s_send.at[2], yrecv.at[0], dev(x, near, core, z, 1 - yl))
    send(here, here, s_send.at[2], yrecv.at[1], dev(x, near, core, z, yl))

    def sideways(n, yh_):
        send(part(x, yh_), part(x, yh_), s_send.at[3], xrecv.at[0, n], to_right)
        send(part(x, yh_), part(x, yh_), s_send.at[3], xrecv.at[1, n], to_left)

    def relay(n, yh_):
        arrived(part(left, yh_), xrecv.at[0, n])
        send(half(0, left, yh_), half(0, left, yh_), s_send.at[4], relay_recv.at[0], to_right)
        arrived(part(right, yh_), xrecv.at[1, n])
        send(half(1, right, yh_), half(1, right, yh_), s_send.at[4], relay_recv.at[1], to_left)

    sideways(0, yh)
    arrived(part(x, near), yrecv.at[0])
    sideways(1, near)
    relay(0, yh)
    arrived(part(x, beside), yrecv.at[1])
    sideways(2, beside)
    arrived(part(x, across), yrecv.at[2])
    send(part(x, across), part(x, across), s_send.at[3], far_recv, to_far)
    sideways(3, across)
    send(line(x), line(x), half_send, half_recv.at[0], core_mate)
    relay(1, near)
    relay(2, beside)
    arrived(part(left, across), xrecv.at[0, 3])
    send(line(left), line(left), half_send, half_recv.at[1], core_mate)
    arrived(part(right, across), xrecv.at[1, 3])
    send(line(right), line(right), half_send, half_recv.at[2], core_mate)
    arrived(part(far, across), far_recv)
    arrived(feats.at[0, pl.ds(0, 3 * PIECE), :], relay_recv.at[0])
    arrived(feats.at[0, pl.ds(0, 3 * PIECE), :], relay_recv.at[1])
    send(line(far), line(far), half_send, half_recv.at[3], core_mate)

    def multiply(t):
        s = lax.rem(2 * core + t, SECTIONS)
        for c in range(RT):
            tiles[c] = feats[s, TILE * c:TILE * c + TILE, :]

        def one(k, carry):
            product = jnp.dot(mask_low[s, k], tiles[tcol[0, 0, s, k]], preferred_element_type=F32)
            sums[1 + t * SLOTS + k] = product + sums[before[t, k]]
            return carry

        lax.fori_loop(0, SLOTS, one, 0, unroll=8)

    multiply(0)
    multiply(1)
    far_half = feats.at[pl.ds(2 * other, 2)]
    for n in range(4):
        arrived(far_half.at[:, pl.ds(0, NYH * PIECE), :], half_recv.at[n])
    multiply(2)
    multiply(3)

    def second_half(step, carry):
        r = lax.rem(lax.div(z, 2) + 1 + step, RT)
        acc[pl.ds(4 * r, 4)] = sums[last[r]].reshape(4, SHARE, F_IN)
        for h in range(2):
            y_out[2 * r + h] = acc[4 * r + 2 * h + 1 - yl].astype(BF16)
        send(y_out.at[pl.ds(2 * r, 2)], y_in.at[pl.ds(2 * r, 2)], yl_send, yl_recv.at[r], yl_mate)
        return carry

    lax.fori_loop(0, RT, second_half, 0)

    def to_z(step, carry):
        r = lax.rem(lax.div(z, 2) + 1 + step, RT)
        arrived(y_in.at[pl.ds(2 * r, 2)], yl_recv.at[r])
        for h in range(2):
            z_ = 2 * r + h
            both = acc[4 * r + 2 * h + yl] + y_in[z_].astype(F32)
            acc[4 * r + 2 * h + yl] = both
            z_out[z_] = both.astype(BF16)

            @pl.when(z_ != z)
            def _():
                send(z_out.at[z_], z_in.at[z], z_send, z_recv, dev(x, yh, core, z_, yl))

        return carry

    lax.fori_loop(0, RT, to_z, 0)
    z_in[z] = jnp.zeros((SHARE, F_IN), BF16)
    lanes = lax.broadcasted_iota(jnp.int32, (SHARE, SHARE), 1)
    subs = lax.broadcasted_iota(jnp.int32, (SHARE, SHARE), 0)
    deg = jnp.sum(jnp.where(lanes == subs, degree[...].astype(F32), 0.0), axis=1, keepdims=True)
    total = acc[2 * z + yl]
    arrived(z_in.at[pl.ds(0, NZ - 1)], z_recv)
    for z_ in range(NZ):
        total = total + z_in[z_].astype(F32)

    mean = (total / deg).astype(BF16)
    pre = pre_own[...] + jnp.dot(mean, w_neigh[...], preferred_element_type=F32)
    fall = jnp.exp(jnp.minimum(pre, 0.0))
    up = pre > 0
    hidden[...] = jnp.where(up, pre, fall - 1.0).astype(BF16)
    grad_pre = cot[...].astype(F32) * jnp.where(up, 1.0, fall)
    grad_low = grad_pre.astype(BF16)
    part_bias = jnp.sum(grad_pre, axis=0, keepdims=True)
    first_core = core == 0
    pair_out[:, 0:F_IN] = jnp.where(first_core, mean, own)
    pair_out[:, F_IN:] = grad_low
    bias_out[...] = jnp.broadcast_to(
        jnp.where(first_core, part_bias[:, F_IN:], part_bias[:, :F_IN]), (8, F_IN)
    )
    send(pair_out, pair_in, g_send.at[0], g_recv.at[0], core_mate)
    send(bias_out, bias_in, g_send.at[1], g_recv.at[1], core_mate)
    over_nodes = (((0,), (0,)), ((), ()))
    part = lax.dot_general(jnp.where(first_core, own, mean), grad_low, over_nodes, preferred_element_type=F32)
    half_bias = jnp.where(first_core, part_bias[:, :F_IN], part_bias[:, F_IN:])
    arrived(pair_in, g_recv.at[0])
    arrived(bias_in, g_recv.at[1])
    part = part + lax.dot_general(
        pair_in[:, 0:F_IN], pair_in[:, F_IN:], over_nodes, preferred_element_type=F32
    )
    bias_tile[...] = half_bias + bias_in[...]
    for o in range(OWNERS):
        m1[o] = part[16 * (o // 2):16 * (o // 2) + 16, TILE * (o % 2):TILE * (o % 2) + TILE].astype(BF16)
    pair_y = lax.div(y, 2)
    me_o = x * (NY // 2) + pair_y
    is_owner = lax.rem(y, 2) == core
    no_owner = lax.rem(y, 2) != core
    is_home = me_q == other
    no_home = me_q != other
    home = at_plane(0, other)
    for dx in (2, 1, 3, 0):
        for k in (2, 1, 3, 0):
            x_, h_ = lax.rem(x + dx, NX), lax.rem(pair_y + k, NY // 2)
            o_, device = x_ * (NY // 2) + h_, at_plane(x_, 2 * h_ + core)
            if dx or k:
                send(m1.at[o_], r1.at[me_q], g_send.at[2], g_recv.at[2], device)
            else:
                @pl.when(no_owner)
                def _():
                    send(m1.at[o_], r1.at[me_q], g_send.at[2], g_recv.at[2], device)

    @pl.when(no_home)
    def _():
        send(bias_tile, rb.at[me_q], g_send.at[7], g_recv.at[7], home)

    far_z = (6, 5, 7, 4, 8, 3, 9, 2, 10, 1, 11)
    norm = float(NODES) ** -0.5

    @pl.when(is_owner)
    def _():
        r1[me_q] = m1[me_o]
        arrived(r1.at[pl.ds(0, NX * NY - 1)], g_recv.at[2])
        level = r1[0].astype(F32)
        for q in range(1, NX * NY):
            level = level + r1[q].astype(F32)
        m3[...] = level.astype(BF16)
        for dz in far_z:
            send(m3, r3.at[z], g_send.at[3], g_recv.at[3], dev(x, yh, core, lax.rem(z + dz, NZ), yl))
        r3[z] = m3[...]
        arrived(r3.at[pl.ds(0, NZ - 1)], g_recv.at[3])
        level = r3[0].astype(F32)
        for k in range(1, NZ):
            level = level + r3[k].astype(F32)
        m4[...] = (level * norm).astype(BF16)
        for x_, y_ in plane:
            send(m4, r4.at[me_o], g_send.at[4], g_recv.at[4], at_plane(x_, y_))
        r4[me_o] = m4[...]
        arrived(r4.at[pl.ds(0, OWNERS - 1)], g_recv.at[4])

    @pl.when(is_home)
    def _():
        rb[me_q] = bias_tile[...]
        arrived(rb.at[pl.ds(0, NX * NY - 1)], g_recv.at[7])
        level = rb[0]
        for q in range(1, NX * NY):
            level = level + rb[q]
        m3b[...] = level
        for dz in far_z:
            send(m3b, r3b.at[z], g_send.at[8], g_recv.at[8], dev(x, yh, core, lax.rem(z + dz, NZ), yl))
        r3b[z] = level
        arrived(r3b.at[pl.ds(0, NZ - 1)], g_recv.at[8])
        level = r3b[0]
        for k in range(1, NZ):
            level = level + r3b[k]
        bias_sum[...] = level * norm
        for x_, y_ in plane:
            send(bias_sum, bias_sum, g_send.at[9], g_recv.at[9], at_plane(x_, y_))

    @pl.when(no_home)
    def _():
        arrived(bias_sum, g_recv.at[9])

    send(bias_sum, bias_far, g_send.at[6], g_recv.at[6], core_mate)

    @pl.when(no_owner)
    def _():
        arrived(r4, g_recv.at[4])

    send(r4, r5, g_send.at[5], g_recv.at[5], core_mate)
    grads[core] = r4[...]

    arrived(owners_v, o_send)
    arrived(got1.at[pl.ds(0, CHIPS - 1)], s_send.at[0])
    arrived(give_core, s_send.at[1])
    arrived(feats.at[0, pl.ds(0, 6 * PIECE), :], s_send.at[2])
    arrived(feats.at[pl.ds(0, 3), pl.ds(0, 6 * PIECE), :], s_send.at[3])
    arrived(feats.at[0, pl.ds(0, 6 * PIECE), :], s_send.at[4])
    arrived(feats.at[pl.ds(0, 2)], half_send)
    arrived(y_out, yl_send)
    arrived(z_out.at[pl.ds(0, NZ - 1)], z_send)
    arrived(pair_out, g_send.at[0])
    arrived(bias_out, g_send.at[1])
    @pl.when(is_owner)
    def _():
        arrived(m1.at[pl.ds(0, OWNERS - 1)], g_send.at[2])
        arrived(r3.at[pl.ds(0, NZ - 1)], g_send.at[3])
        arrived(r1.at[pl.ds(0, NX * NY - 1)], g_send.at[4])

    @pl.when(no_owner)
    def _():
        arrived(m1, g_send.at[2])

    @pl.when(is_home)
    def _():
        arrived(r3b.at[pl.ds(0, NZ - 1)], g_send.at[8])
        arrived(rb.at[pl.ds(0, NX * NY - 1)], g_send.at[9])

    @pl.when(no_home)
    def _():
        arrived(bias_tile, g_send.at[7])

    arrived(bias_sum, g_send.at[6])
    arrived(r4, g_send.at[5])

    arrived(bias_far, g_recv.at[6])
    near_bias, far_bias = bias_sum[0:1, :], bias_far[0:1, :]
    g_bias[:, 0:F_IN] = jnp.where(first_core, near_bias, far_bias)
    g_bias[:, F_IN:] = jnp.where(first_core, far_bias, near_bias)
    arrived(r5, g_recv.at[5])
    grads[other] = r5[...]


def spread(hidden_in, grads_h, bias_in, hidden, g_self, g_neigh, g_bias, grads_in, sems):
    moves = [
        pltpu.make_async_copy(a, b, sems.at[n])
        for n, (a, b) in enumerate(((grads_h, grads_in), (hidden_in, hidden), (bias_in, g_bias)))
    ]
    for move in moves:
        move.start()
    moves[0].wait()
    for half, target in enumerate((g_self, g_neigh)):
        for o in range(OWNERS):
            target[16 * (o // 2):16 * (o // 2) + 16, TILE * (o % 2):TILE * (o % 2) + TILE] = grads_in[
                half, o
            ].astype(F32)
    moves[1].wait()
    moves[2].wait()


def body(
    features, self_weight, neigh_weight, bias, degree, cotangent, owners, tile_rows, tile_cols, tile_count, masks
):
    vmem = pl.BlockSpec(memory_space=pltpu.VMEM)
    dma = pltpu.SemaphoreType.DMA
    hidden, grads, g_bias = pl.pallas_call(
        kernel,
        out_shape=(
            jax.ShapeDtypeStruct((SHARE, F), BF16),
            jax.ShapeDtypeStruct((NC, OWNERS, 16, TILE), BF16),
            jax.ShapeDtypeStruct((1, F), F32),
        ),
        in_specs=[pl.BlockSpec(memory_space=pl.ANY)] * 11,
        out_specs=(vmem,) * 3,
        scratch_shapes=[
            pltpu.VMEM((ROWS, F_IN), BF16),
            pltpu.VMEM((F_IN, F), BF16),
            pltpu.VMEM((F_IN, F), BF16),
            pltpu.VMEM((1, F), F32),
            pltpu.VMEM((1, SHARE), jnp.int32),
            pltpu.VMEM((SHARE, F), BF16),
            pltpu.SMEM((1, SECTIONS), jnp.int32),
            pltpu.VMEM((1, SECTIONS), jnp.int32),
            pltpu.VMEM((1, SECTIONS), jnp.int32),
            pltpu.SMEM((1, SECTIONS), jnp.int32),
            pltpu.SMEM((1, 1, SECTIONS, SLOTS), jnp.int32),
            pltpu.SMEM((1, 1, SECTIONS, SLOTS), jnp.int32),
            pltpu.SMEM((1, 1, SECTIONS), jnp.int32),
            pltpu.SMEM((SECTIONS, SLOTS), jnp.int32),
            pltpu.SMEM((RT,), jnp.int32),
            pltpu.VMEM((SECTIONS, SLOTS, TILE, TILE), jnp.int32),
            pltpu.VMEM((SECTIONS, SLOTS, TILE, TILE), BF16),
            pltpu.VMEM((CHIPS, PIECE, F_IN), BF16),
            pltpu.VMEM((2, 2, PIECE, F_IN), BF16),
            pltpu.VMEM((2, 2, PIECE, F_IN), BF16),
            pltpu.VMEM((SECTIONS, ROWS, F_IN), BF16),
            pltpu.VMEM((2, PIECE, F_IN), BF16),
            pltpu.VMEM((RT, TILE, F_IN), BF16),
            pltpu.VMEM((1 + SECTIONS * SLOTS, TILE, F_IN), F32),
            pltpu.VMEM((NZ * NYL, SHARE, F_IN), F32),
            pltpu.VMEM((NZ, SHARE, F_IN), BF16),
            pltpu.VMEM((NZ, SHARE, F_IN), BF16),
            pltpu.VMEM((NZ, SHARE, F_IN), BF16),
            pltpu.VMEM((NZ, SHARE, F_IN), BF16),
            pltpu.VMEM((SHARE, F), F32),
            pltpu.VMEM((SHARE, F_IN + F), BF16),
            pltpu.VMEM((SHARE, F_IN + F), BF16),
            pltpu.VMEM((8, F_IN), F32),
            pltpu.VMEM((8, F_IN), F32),
            pltpu.VMEM((8, F_IN), F32),
            pltpu.VMEM((8, F_IN), F32),
            pltpu.VMEM((OWNERS, 16, TILE), BF16),
            pltpu.VMEM((NX * NY, 16, TILE), BF16),
            pltpu.VMEM((16, TILE), BF16),
            pltpu.VMEM((NZ, 16, TILE), BF16),
            pltpu.VMEM((16, TILE), BF16),
            pltpu.VMEM((OWNERS, 16, TILE), BF16),
            pltpu.VMEM((OWNERS, 16, TILE), BF16),
            pltpu.VMEM((8, TILE), F32),
            pltpu.VMEM((NX * NY, 8, TILE), F32),
            pltpu.VMEM((8, TILE), F32),
            pltpu.VMEM((NZ, 8, TILE), F32),
            dma((11,)),
            dma((SECTIONS,)),
            dma,
            dma,
            dma,
            dma((5,)),
            dma,
            dma,
            dma((3,)),
            dma((2, NYH)),
            dma,
            dma((2,)),
            dma,
            dma((4,)),
            dma,
            dma((RT,)),
            dma,
            dma,
            dma((10,)),
            dma((10,)),
        ],
        compiler_params=pltpu.CompilerParams(
            collective_id=0, has_side_effects=True, vmem_limit_bytes=60 * 1024 * 1024
        ),
    )(
        features, self_weight, neigh_weight, bias.reshape(1, F), degree.reshape(1, SHARE), cotangent,
        owners, tile_rows, tile_cols, tile_count, masks.reshape(SECTIONS, SLOTS, TILE, TILE),
    )
    hidden, g_self, g_neigh, g_bias = pl.pallas_call(
        spread,
        out_shape=(
            jax.ShapeDtypeStruct((SHARE, F), BF16),
            jax.ShapeDtypeStruct((F_IN, F), F32),
            jax.ShapeDtypeStruct((F_IN, F), F32),
            jax.ShapeDtypeStruct((1, F), F32),
        ),
        in_specs=[pl.BlockSpec(memory_space=pl.ANY)] * 3,
        out_specs=(
            pl.BlockSpec(memory_space=pl.ANY), vmem, vmem, pl.BlockSpec(memory_space=pl.ANY)
        ),
        scratch_shapes=[pltpu.VMEM((NC, OWNERS, 16, TILE), BF16), pltpu.SemaphoreType.DMA((3,))],
        compiler_params=pltpu.CompilerParams(vmem_limit_bytes=60 * 1024 * 1024),
    )(hidden, grads, g_bias)
    return hidden, g_self, g_neigh, g_bias.reshape(F)


def solution(mesh):
    return jax.shard_map(
        body,
        mesh=mesh,
        in_specs=(
            P("rows", None),
            P(),
            P(),
            P(),
            P(("rows", "rep")),
            P(("rows", "rep"), None),
            P("rep", None),
            P("rows", "rep", None, None),
            P("rows", "rep", None, None),
            P("rows", "rep", None),
            P("rows", "rep", None, None, None, None),
        ),
        out_specs=(P(("rows", "rep"), None), P(), P(), P()),
        check_vma=False,
    )
```

```python
import functools

import jax
import jax.numpy as jnp
from jax import lax
from jax.experimental import pallas as pl
from jax.experimental.pallas import tpu as pltpu
from jax.sharding import PartitionSpec as P

MESH = pl.DeviceIdType.MESH
NX, NYH, NC, NZ, NYL = 4, 4, 2, 12, 2
NY = NYH * NYL
TILE = 128
RT = 6
SECTIONS = 4
SLOTS = 16
ROWS = 768
CHIPS = NX * NYH
PIECE = ROWS // CHIPS
SHARE = ROWS // (NZ * NYL)
OWNERS = NX * NY // 2
F_IN = 128
F = 256
NODES = 24576
F32 = jnp.float32
BF16 = jnp.bfloat16


def kernel(
    feat_h, w_self_h, w_neigh_h, bias_h, degree_h, cot_h, owners_h, trow_h, tcol_h, tcnt_h, masks,
    hidden, grads, g_bias,
    feat, w_self, w_neigh, bias, degree, cot, owners, owners_v, owners_mate_v, owners_mate, trow, tcol, tcnt,
    before, last, mask_raw, mask_low, got1, give_core, got_core, feats, part_mate, tiles, sums, acc, y_out, y_in,
    z_out, z_in, pre_own, pair_out, pair_in, bias_out, bias_in, bias_sum, bias_far,
    m1, r1, m3, r3, m4, r4, r5, bias_tile, rb, m3b, r3b,
    in_sem, mask_sem, o_send, o_recv, o_copy, s_send, s1_recv, core_recv, yrecv, xrecv, half_send, half_recv,
    yl_send, yl_recv, z_send, z_recv, g_send, g_recv,
):
    row, rep = lax.axis_index("rows"), lax.axis_index("rep")
    core = lax.rem(row, NC)
    chip = lax.div(row, NC)
    yh = lax.rem(chip, NYH)
    x = lax.div(chip, NYH)
    yl = lax.rem(rep, NYL)
    z = lax.div(rep, NYL)
    y = yh * NYL + yl
    other = 1 - core

    def dev(x_, yh_, c_, z_, yl_):
        return ((x_ * NYH + yh_) * NC + c_, z_ * NYL + yl_)

    def at_plane(x_, y_):
        return dev(x_, lax.div(y_, NYL), core, z, lax.rem(y_, NYL))

    def send(src, dst, ssem, rsem, device):
        copy = pltpu.make_async_remote_copy(
            src_ref=src, dst_ref=dst, send_sem=ssem, recv_sem=rsem, device_id=device, device_id_type=MESH
        )
        copy.start()

    def arrived(buf, sem):
        pltpu.make_async_copy(buf, buf, sem).wait()

    core_mate = dev(x, yh, other, z, yl)
    yl_mate = dev(x, yh, core, z, 1 - yl)
    plane = [(lax.rem(x + dx, NX), lax.rem(y + dy, NY)) for dx in (2, 1, 3, 0) for dy in (4, 3, 5, 2, 6, 1, 7, 0)]
    plane = plane[:-1]
    me_q = x * NY + y

    pairs = (
        (feat_h, feat), (owners_h, owners_v), (owners_h, owners), (w_self_h, w_self), (bias_h, bias), (trow_h, trow), (tcol_h, tcol),
        (tcnt_h, tcnt), (w_neigh_h, w_neigh), (degree_h, degree), (cot_h, cot),
    )
    loads = [pltpu.make_async_copy(a, b, in_sem.at[n]) for n, (a, b) in enumerate(pairs)]
    loads[0].start()
    barrier = pltpu.get_barrier_semaphore()

    def greet(device):
        pl.semaphore_signal(barrier, inc=1, device_id=device, device_id_type=MESH)

    for dz in (6, 5, 7, 4, 8, 3, 9, 2, 10, 1, 11):
        greet(dev(x, yh, core, lax.rem(z + dz, NZ), yl))
    for x_, y_ in plane:
        greet(at_plane(x_, y_))
    greet(core_mate)

    for copy in loads[1:]:
        copy.start()
    mask_copies = [
        pltpu.make_async_copy(masks.at[s], mask_raw.at[s], mask_sem.at[s]) for s in range(SECTIONS)
    ]
    for copy in mask_copies:
        copy.start()
    loads[0].wait()
    loads[1].wait()
    loads[2].wait()
    got1[chip] = feat[pl.ds(pl.multiple_of(chip * PIECE, 16), PIECE), :]
    pl.semaphore_wait(barrier, len(plane) + NZ)

    send(owners_v, owners_mate_v, o_send, o_recv, yl_mate)
    near, across = lax.rem(yh + 2 * yl + NYH - 1, NYH), lax.rem(yh + 2, NYH)
    shares = [(2, across, 1 - yl), (1, across, 1 - yl), (3, across, 1 - yl), (0, across, 1 - yl)]
    shares += [(dx, near, yl_) for dx in (2, 1, 3, 0) for yl_ in range(NYL)]
    shares += [(dx, yh, yl) for dx in (2, 1, 3)]
    for dx, yh_, yl_ in shares:
        x_ = lax.rem(x + dx, NX)
        there = x_ * NYH + yh_
        send(
            feat.at[pl.ds(pl.multiple_of(there * PIECE, 16), PIECE), :],
            got1.at[chip], s_send.at[0], s1_recv, dev(x_, yh_, core, z, yl_),
        )

    for copy in loads[3:]:
        copy.wait()
    own = feat[pl.ds(pl.multiple_of(rep * SHARE, 16), SHARE), :]
    pre_own[...] = jnp.dot(own, w_self[...], preferred_element_type=F32) + bias[...]
    for s in range(SECTIONS):
        mask_copies[s].wait()

        def lower(k, carry, s=s):
            mask_low[s, k] = mask_raw[s, k].astype(F32).astype(BF16)
            return carry

        lax.fori_loop(0, SLOTS, lower, 0, unroll=2)

    def chain(t, ends):
        s = lax.rem(2 * core + t, SECTIONS)
        count = tcnt[0, 0, s]
        ends = list(ends)
        for k in range(SLOTS):
            live = jnp.minimum(jnp.maximum(count - k, 0), 1)
            spot = 1 + t * SLOTS + k
            link = 0
            for r in range(RT):
                gap = trow[0, 0, s, k] - r
                same = live * (1 - jnp.minimum(gap * gap, 1))
                link = link + same * ends[r]
                ends[r] = ends[r] + same * (spot - ends[r])
            before[t, k] = link
        return tuple(ends)

    ends = lax.fori_loop(0, SECTIONS, chain, (jnp.int32(0),) * RT)
    for r in range(RT):
        last[r] = ends[r]
    sums[0] = jnp.zeros((TILE, F_IN), F32)
    arrived(owners_mate_v, o_recv)
    fetch = pltpu.make_async_copy(owners_mate_v, owners_mate, o_copy)
    fetch.start()
    fetch.wait()
    arrived(got1.at[pl.ds(0, CHIPS - 1)], s1_recv)

    def chosen(table, s):
        owner = table[0, s]
        piece = jnp.zeros((PIECE, F_IN), F32)
        for b in range(CHIPS):
            gap = owner - (NC * b + core)
            piece = piece + got1[b].astype(F32) * (1 - jnp.minimum(gap * gap, 1)).astype(F32)
        return piece

    for t in range(2):
        give_core[0, t] = chosen(owners, 2 * other + t).astype(BF16)
        give_core[1, t] = chosen(owners_mate, 2 * other + t).astype(BF16)
    send(give_core, got_core, s_send.at[1], core_recv, core_mate)
    mine = [chosen(table, 2 * core + t) for table in (owners, owners_mate) for t in range(2)]
    arrived(got_core, core_recv)
    place = pl.ds(pl.multiple_of(chip * PIECE, 16), PIECE)
    for t in range(2):
        feats[2 * core + t, place, :] = (mine[t] + got_core[0, t].astype(F32)).astype(BF16)
        part_mate[t] = (mine[2 + t] + got_core[1, t].astype(F32)).astype(BF16)

    here = feats.at[pl.ds(2 * core, 2), place, :]

    def line(x_):
        start = pl.multiple_of(x_ * (NYH * PIECE), 16)
        return feats.at[pl.ds(2 * core, 2), pl.ds(start, NYH * PIECE), :]

    def part(x_, yh_):
        start = pl.multiple_of((x_ * NYH + yh_) * PIECE, 16)
        return feats.at[pl.ds(2 * core, 2), pl.ds(start, PIECE), :]

    right, left, far = lax.rem(x + 1, NX), lax.rem(x + 3, NX), lax.rem(x + 2, NX)
    to_right, to_left, to_far = (dev(x_, yh, core, z, yl) for x_ in (right, left, far))
    beside = lax.rem(yh + 1 - 2 * yl + NYH, NYH)
    send(part_mate, here, s_send.at[2], yrecv.at[2], dev(x, across, core, z, 1 - yl))
    send(part_mate, here, s_send.at[2], yrecv.at[0], dev(x, near, core, z, 1 - yl))
    send(here, here, s_send.at[2], yrecv.at[1], dev(x, near, core, z, yl))

    def sideways(n, yh_):
        for k, device in enumerate((to_far, to_right, to_left)):
            send(part(x, yh_), part(x, yh_), s_send.at[3], xrecv.at[k], device)

    sideways(0, yh)
    arrived(part(x, near), yrecv.at[0])
    sideways(1, near)
    arrived(part(x, beside), yrecv.at[1])
    sideways(2, beside)
    arrived(part(x, across), yrecv.at[2])
    sideways(3, across)
    send(line(x), line(x), half_send, half_recv.at[0], core_mate)
    for n, source in ((1, left), (2, right), (0, far)):
        arrived(line(source), xrecv.at[n])
        send(line(source), line(source), half_send, half_recv.at[n or 3], core_mate)

    def multiply(t):
        s = lax.rem(2 * core + t, SECTIONS)
        for c in range(RT):
            tiles[c] = feats[s, TILE * c:TILE * c + TILE, :]

        def one(k, carry):
            product = jnp.dot(mask_low[s, k], tiles[tcol[0, 0, s, k]], preferred_element_type=F32)
            sums[1 + t * SLOTS + k] = product + sums[before[t, k]]
            return carry

        lax.fori_loop(0, SLOTS, one, 0, unroll=8)

    multiply(0)
    multiply(1)
    far_half = feats.at[pl.ds(2 * other, 2)]
    for n in range(4):
        arrived(far_half.at[:, pl.ds(0, NYH * PIECE), :], half_recv.at[n])
    multiply(2)
    multiply(3)

    order = [lax.rem(lax.div(z, 2) + step, RT) for step in (3, 2, 4, 1, 5, 0)]
    for r in order:
        acc[pl.ds(4 * r, 4)] = sums[last[r]].reshape(4, SHARE, F_IN)
        for h in range(2):
            y_out[2 * r + h] = acc[4 * r + 2 * h + 1 - yl].astype(BF16)
        send(y_out.at[pl.ds(2 * r, 2)], y_in.at[pl.ds(2 * r, 2)], yl_send, yl_recv.at[r], yl_mate)

    for step, r in enumerate(order):
        arrived(y_in.at[pl.ds(2 * r, 2)], yl_recv.at[r])
        for h in range(2):
            z_ = 2 * r + h
            both = acc[4 * r + 2 * h + yl] + y_in[z_].astype(F32)
            acc[4 * r + 2 * h + yl] = both
            z_out[z_] = both.astype(BF16)
            if step < RT - 1:
                send(z_out.at[z_], z_in.at[z], z_send, z_recv, dev(x, yh, core, z_, yl))
            else:
                @pl.when(z_ != z)
                def _(z_=z_):
                    send(z_out.at[z_], z_in.at[z], z_send, z_recv, dev(x, yh, core, z_, yl))

    z_in[z] = jnp.zeros((SHARE, F_IN), BF16)
    lanes = lax.broadcasted_iota(jnp.int32, (SHARE, SHARE), 1)
    subs = lax.broadcasted_iota(jnp.int32, (SHARE, SHARE), 0)
    deg = jnp.sum(jnp.where(lanes == subs, degree[...].astype(F32), 0.0), axis=1, keepdims=True)
    total = acc[2 * z + yl]
    arrived(z_in.at[pl.ds(0, NZ - 1)], z_recv)
    for z_ in range(NZ):
        total = total + z_in[z_].astype(F32)

    mean = (total / deg).astype(BF16)
    pre = pre_own[...] + jnp.dot(mean, w_neigh[...], preferred_element_type=F32)
    fall = jnp.exp(jnp.minimum(pre, 0.0))
    up = pre > 0
    hidden[...] = jnp.where(up, pre, fall - 1.0).astype(BF16)
    grad_pre = cot[...].astype(F32) * jnp.where(up, 1.0, fall)
    grad_low = grad_pre.astype(BF16)
    part_bias = jnp.sum(grad_pre, axis=0, keepdims=True)
    first_core = core == 0
    pair_out[:, 0:F_IN] = jnp.where(first_core, mean, own)
    pair_out[:, F_IN:] = grad_low
    bias_out[...] = jnp.broadcast_to(
        jnp.where(first_core, part_bias[:, F_IN:], part_bias[:, :F_IN]), (8, F_IN)
    )
    send(pair_out, pair_in, g_send.at[0], g_recv.at[0], core_mate)
    send(bias_out, bias_in, g_send.at[1], g_recv.at[1], core_mate)
    over_nodes = (((0,), (0,)), ((), ()))
    part = lax.dot_general(jnp.where(first_core, own, mean), grad_low, over_nodes, preferred_element_type=F32)
    half_bias = jnp.where(first_core, part_bias[:, :F_IN], part_bias[:, F_IN:])
    arrived(pair_in, g_recv.at[0])
    arrived(bias_in, g_recv.at[1])
    part = part + lax.dot_general(
        pair_in[:, 0:F_IN], pair_in[:, F_IN:], over_nodes, preferred_element_type=F32
    )
    bias_tile[...] = half_bias + bias_in[...]
    for o in range(OWNERS):
        m1[o] = part[16 * (o // 2):16 * (o // 2) + 16, TILE * (o % 2):TILE * (o % 2) + TILE].astype(BF16)
    pair_y = lax.div(y, 2)
    me_o = x * (NY // 2) + pair_y
    is_owner = lax.rem(y, 2) == core
    no_owner = lax.rem(y, 2) != core
    is_home = me_q == other
    no_home = me_q != other
    home = at_plane(0, other)
    for dx in (2, 1, 3, 0):
        for k in (2, 1, 3, 0):
            x_, h_ = lax.rem(x + dx, NX), lax.rem(pair_y + k, NY // 2)
            o_, device = x_ * (NY // 2) + h_, at_plane(x_, 2 * h_ + core)
            if dx or k:
                send(m1.at[o_], r1.at[me_q], g_send.at[2], g_recv.at[2], device)
            else:
                @pl.when(no_owner)
                def _():
                    send(m1.at[o_], r1.at[me_q], g_send.at[2], g_recv.at[2], device)

    @pl.when(no_home)
    def _():
        send(bias_tile, rb.at[me_q], g_send.at[7], g_recv.at[7], home)

    far_z = (6, 5, 7, 4, 8, 3, 9, 2, 10, 1, 11)
    norm = float(NODES) ** -0.5

    @pl.when(is_owner)
    def _():
        r1[me_q] = m1[me_o]
        arrived(r1.at[pl.ds(0, NX * NY - 1)], g_recv.at[2])
        level = r1[0].astype(F32)
        for q in range(1, NX * NY):
            level = level + r1[q].astype(F32)
        m3[...] = level.astype(BF16)
        for dz in far_z:
            send(m3, r3.at[z], g_send.at[3], g_recv.at[3], dev(x, yh, core, lax.rem(z + dz, NZ), yl))
        r3[z] = m3[...]
        arrived(r3.at[pl.ds(0, NZ - 1)], g_recv.at[3])
        level = r3[0].astype(F32)
        for k in range(1, NZ):
            level = level + r3[k].astype(F32)
        m4[...] = (level * norm).astype(BF16)
        for x_, y_ in plane:
            send(m4, r4.at[me_o], g_send.at[4], g_recv.at[4], at_plane(x_, y_))
        r4[me_o] = m4[...]
        arrived(r4.at[pl.ds(0, OWNERS - 1)], g_recv.at[4])

    @pl.when(is_home)
    def _():
        rb[me_q] = bias_tile[...]
        arrived(rb.at[pl.ds(0, NX * NY - 1)], g_recv.at[7])
        level = rb[0]
        for q in range(1, NX * NY):
            level = level + rb[q]
        m3b[...] = level
        for dz in far_z:
            send(m3b, r3b.at[z], g_send.at[8], g_recv.at[8], dev(x, yh, core, lax.rem(z + dz, NZ), yl))
        r3b[z] = level
        arrived(r3b.at[pl.ds(0, NZ - 1)], g_recv.at[8])
        level = r3b[0]
        for k in range(1, NZ):
            level = level + r3b[k]
        bias_sum[...] = level * norm
        for x_, y_ in plane:
            send(bias_sum, bias_sum, g_send.at[9], g_recv.at[9], at_plane(x_, y_))

    @pl.when(no_home)
    def _():
        arrived(bias_sum, g_recv.at[9])

    send(bias_sum, bias_far, g_send.at[6], g_recv.at[6], core_mate)

    @pl.when(no_owner)
    def _():
        arrived(r4, g_recv.at[4])

    send(r4, r5, g_send.at[5], g_recv.at[5], core_mate)
    grads[core] = r4[...]

    arrived(owners_v, o_send)
    arrived(got1.at[pl.ds(0, CHIPS - 1)], s_send.at[0])
    arrived(give_core, s_send.at[1])
    arrived(feats.at[0, pl.ds(0, 6 * PIECE), :], s_send.at[2])
    arrived(feats.at[pl.ds(0, 3), pl.ds(0, 8 * PIECE), :], s_send.at[3])
    arrived(feats.at[pl.ds(0, 2)], half_send)
    arrived(y_out, yl_send)
    arrived(z_out.at[pl.ds(0, NZ - 1)], z_send)
    arrived(pair_out, g_send.at[0])
    arrived(bias_out, g_send.at[1])
    @pl.when(is_owner)
    def _():
        arrived(m1.at[pl.ds(0, OWNERS - 1)], g_send.at[2])
        arrived(r3.at[pl.ds(0, NZ - 1)], g_send.at[3])
        arrived(r1.at[pl.ds(0, NX * NY - 1)], g_send.at[4])

    @pl.when(no_owner)
    def _():
        arrived(m1, g_send.at[2])

    @pl.when(is_home)
    def _():
        arrived(r3b.at[pl.ds(0, NZ - 1)], g_send.at[8])
        arrived(rb.at[pl.ds(0, NX * NY - 1)], g_send.at[9])

    @pl.when(no_home)
    def _():
        arrived(bias_tile, g_send.at[7])

    arrived(bias_sum, g_send.at[6])
    arrived(r4, g_send.at[5])

    arrived(bias_far, g_recv.at[6])
    near_bias, far_bias = bias_sum[0:1, :], bias_far[0:1, :]
    g_bias[:, 0:F_IN] = jnp.where(first_core, near_bias, far_bias)
    g_bias[:, F_IN:] = jnp.where(first_core, far_bias, near_bias)
    arrived(r5, g_recv.at[5])
    grads[other] = r5[...]


def spread(hidden_in, grads_h, bias_in, hidden, g_self, g_neigh, g_bias, grads_in, sems):
    moves = [
        pltpu.make_async_copy(a, b, sems.at[n])
        for n, (a, b) in enumerate(((grads_h, grads_in), (hidden_in, hidden), (bias_in, g_bias)))
    ]
    for move in moves:
        move.start()
    moves[0].wait()
    for half, target in enumerate((g_self, g_neigh)):
        for o in range(OWNERS):
            target[16 * (o // 2):16 * (o // 2) + 16, TILE * (o % 2):TILE * (o % 2) + TILE] = grads_in[
                half, o
            ].astype(F32)
    moves[1].wait()
    moves[2].wait()


def body(
    features, self_weight, neigh_weight, bias, degree, cotangent, owners, tile_rows, tile_cols, tile_count, masks
):
    vmem = pl.BlockSpec(memory_space=pltpu.VMEM)
    dma = pltpu.SemaphoreType.DMA
    hidden, grads, g_bias = pl.pallas_call(
        kernel,
        out_shape=(
            jax.ShapeDtypeStruct((SHARE, F), BF16),
            jax.ShapeDtypeStruct((NC, OWNERS, 16, TILE), BF16),
            jax.ShapeDtypeStruct((1, F), F32),
        ),
        in_specs=[pl.BlockSpec(memory_space=pl.ANY)] * 11,
        out_specs=(vmem,) * 3,
        scratch_shapes=[
            pltpu.VMEM((ROWS, F_IN), BF16),
            pltpu.VMEM((F_IN, F), BF16),
            pltpu.VMEM((F_IN, F), BF16),
            pltpu.VMEM((1, F), F32),
            pltpu.VMEM((1, SHARE), jnp.int32),
            pltpu.VMEM((SHARE, F), BF16),
            pltpu.SMEM((1, SECTIONS), jnp.int32),
            pltpu.VMEM((1, SECTIONS), jnp.int32),
            pltpu.VMEM((1, SECTIONS), jnp.int32),
            pltpu.SMEM((1, SECTIONS), jnp.int32),
            pltpu.SMEM((1, 1, SECTIONS, SLOTS), jnp.int32),
            pltpu.SMEM((1, 1, SECTIONS, SLOTS), jnp.int32),
            pltpu.SMEM((1, 1, SECTIONS), jnp.int32),
            pltpu.SMEM((SECTIONS, SLOTS), jnp.int32),
            pltpu.SMEM((RT,), jnp.int32),
            pltpu.VMEM((SECTIONS, SLOTS, TILE, TILE), jnp.int32),
            pltpu.VMEM((SECTIONS, SLOTS, TILE, TILE), BF16),
            pltpu.VMEM((CHIPS, PIECE, F_IN), BF16),
            pltpu.VMEM((2, 2, PIECE, F_IN), BF16),
            pltpu.VMEM((2, 2, PIECE, F_IN), BF16),
            pltpu.VMEM((SECTIONS, ROWS, F_IN), BF16),
            pltpu.VMEM((2, PIECE, F_IN), BF16),
            pltpu.VMEM((RT, TILE, F_IN), BF16),
            pltpu.VMEM((1 + SECTIONS * SLOTS, TILE, F_IN), F32),
            pltpu.VMEM((NZ * NYL, SHARE, F_IN), F32),
            pltpu.VMEM((NZ, SHARE, F_IN), BF16),
            pltpu.VMEM((NZ, SHARE, F_IN), BF16),
            pltpu.VMEM((NZ, SHARE, F_IN), BF16),
            pltpu.VMEM((NZ, SHARE, F_IN), BF16),
            pltpu.VMEM((SHARE, F), F32),
            pltpu.VMEM((SHARE, F_IN + F), BF16),
            pltpu.VMEM((SHARE, F_IN + F), BF16),
            pltpu.VMEM((8, F_IN), F32),
            pltpu.VMEM((8, F_IN), F32),
            pltpu.VMEM((8, F_IN), F32),
            pltpu.VMEM((8, F_IN), F32),
            pltpu.VMEM((OWNERS, 16, TILE), BF16),
            pltpu.VMEM((NX * NY, 16, TILE), BF16),
            pltpu.VMEM((16, TILE), BF16),
            pltpu.VMEM((NZ, 16, TILE), BF16),
            pltpu.VMEM((16, TILE), BF16),
            pltpu.VMEM((OWNERS, 16, TILE), BF16),
            pltpu.VMEM((OWNERS, 16, TILE), BF16),
            pltpu.VMEM((8, TILE), F32),
            pltpu.VMEM((NX * NY, 8, TILE), F32),
            pltpu.VMEM((8, TILE), F32),
            pltpu.VMEM((NZ, 8, TILE), F32),
            dma((11,)),
            dma((SECTIONS,)),
            dma,
            dma,
            dma,
            dma((4,)),
            dma,
            dma,
            dma((3,)),
            dma((3,)),
            dma,
            dma((4,)),
            dma,
            dma((RT,)),
            dma,
            dma,
            dma((10,)),
            dma((10,)),
        ],
        compiler_params=pltpu.CompilerParams(
            collective_id=0, has_side_effects=True, vmem_limit_bytes=60 * 1024 * 1024
        ),
    )(
        features, self_weight, neigh_weight, bias.reshape(1, F), degree.reshape(1, SHARE), cotangent,
        owners, tile_rows, tile_cols, tile_count, masks.reshape(SECTIONS, SLOTS, TILE, TILE),
    )
    hidden, g_self, g_neigh, g_bias = pl.pallas_call(
        spread,
        out_shape=(
            jax.ShapeDtypeStruct((SHARE, F), BF16),
            jax.ShapeDtypeStruct((F_IN, F), F32),
            jax.ShapeDtypeStruct((F_IN, F), F32),
            jax.ShapeDtypeStruct((1, F), F32),
        ),
        in_specs=[pl.BlockSpec(memory_space=pl.ANY)] * 3,
        out_specs=(
            pl.BlockSpec(memory_space=pl.ANY), vmem, vmem, pl.BlockSpec(memory_space=pl.ANY)
        ),
        scratch_shapes=[pltpu.VMEM((NC, OWNERS, 16, TILE), BF16), pltpu.SemaphoreType.DMA((3,))],
        compiler_params=pltpu.CompilerParams(vmem_limit_bytes=60 * 1024 * 1024),
    )(hidden, grads, g_bias)
    return hidden, g_self, g_neigh, g_bias.reshape(F)


def solution(mesh):
    return jax.shard_map(
        body,
        mesh=mesh,
        in_specs=(
            P("rows", None),
            P(),
            P(),
            P(),
            P(("rows", "rep")),
            P(("rows", "rep"), None),
            P("rep", None),
            P("rows", "rep", None, None),
            P("rows", "rep", None, None),
            P("rows", "rep", None),
            P("rows", "rep", None, None, None, None),
        ),
        out_specs=(P(("rows", "rep"), None), P(), P(), P()),
        check_vma=False,
    )
```

```python
import functools

import jax
import jax.numpy as jnp
from jax import lax
from jax.experimental import pallas as pl
from jax.experimental.pallas import tpu as pltpu
from jax.sharding import PartitionSpec as P

MESH = pl.DeviceIdType.MESH
NX, NYH, NC, NZ, NYL = 4, 4, 2, 12, 2
NY = NYH * NYL
TILE = 128
RT = 6
SECTIONS = 4
SLOTS = 16
ROWS = 768
CHIPS = NX * NYH
PIECE = ROWS // CHIPS
SHARE = ROWS // (NZ * NYL)
OWNERS = NX * NY // 2
F_IN = 128
F = 256
NODES = 24576
F32 = jnp.float32
BF16 = jnp.bfloat16


def kernel(
    feat_h, w_self_h, w_neigh_h, bias_h, degree_h, cot_h, owners_h, trow_h, tcol_h, tcnt_h, masks,
    hidden, grads, g_bias,
    feat, w_self, w_neigh, bias, degree, cot, owners, owners_v, owners_mate_v, owners_mate, trow, tcol, tcnt,
    before, last, mask_raw, mask_low, got1, give_core, got_core, feats, part_mate, tiles, prods, sums, acc, y_out, y_in,
    z_out, z_in, pre_own, pair_out, pair_in, bias_out, bias_in, bias_sum, bias_far,
    m1, r1, m3, r3, m4, r4, r5, bias_tile, rb, m3b, r3b,
    in_sem, mask_sem, o_send, o_recv, o_copy, s_send, s1_recv, core_recv, yrecv, xrecv, half_send, half_recv,
    yl_send, yl_recv, z_send, z_recv, g_send, g_recv,
):
    row, rep = lax.axis_index("rows"), lax.axis_index("rep")
    core = lax.rem(row, NC)
    chip = lax.div(row, NC)
    yh = lax.rem(chip, NYH)
    x = lax.div(chip, NYH)
    yl = lax.rem(rep, NYL)
    z = lax.div(rep, NYL)
    y = yh * NYL + yl
    other = 1 - core

    def dev(x_, yh_, c_, z_, yl_):
        return ((x_ * NYH + yh_) * NC + c_, z_ * NYL + yl_)

    def at_plane(x_, y_):
        return dev(x_, lax.div(y_, NYL), core, z, lax.rem(y_, NYL))

    def send(src, dst, ssem, rsem, device):
        copy = pltpu.make_async_remote_copy(
            src_ref=src, dst_ref=dst, send_sem=ssem, recv_sem=rsem, device_id=device, device_id_type=MESH
        )
        copy.start()

    def arrived(buf, sem):
        pltpu.make_async_copy(buf, buf, sem).wait()

    core_mate = dev(x, yh, other, z, yl)
    yl_mate = dev(x, yh, core, z, 1 - yl)
    plane = [(lax.rem(x + dx, NX), lax.rem(y + dy, NY)) for dx in (2, 1, 3, 0) for dy in (4, 3, 5, 2, 6, 1, 7, 0)]
    plane = plane[:-1]
    me_q = x * NY + y

    pairs = (
        (feat_h, feat), (owners_h, owners_v), (owners_h, owners), (w_self_h, w_self), (bias_h, bias), (trow_h, trow), (tcol_h, tcol),
        (tcnt_h, tcnt), (w_neigh_h, w_neigh), (degree_h, degree), (cot_h, cot),
    )
    loads = [pltpu.make_async_copy(a, b, in_sem.at[n]) for n, (a, b) in enumerate(pairs)]
    loads[0].start()
    barrier = pltpu.get_barrier_semaphore()

    def greet(device):
        pl.semaphore_signal(barrier, inc=1, device_id=device, device_id_type=MESH)

    for dz in (6, 5, 7, 4, 8, 3, 9, 2, 10, 1, 11):
        greet(dev(x, yh, core, lax.rem(z + dz, NZ), yl))
    for x_, y_ in plane:
        greet(at_plane(x_, y_))
    greet(core_mate)

    for copy in loads[1:]:
        copy.start()
    mask_copies = [
        pltpu.make_async_copy(masks.at[s], mask_raw.at[s], mask_sem.at[s]) for s in range(SECTIONS)
    ]
    for copy in mask_copies:
        copy.start()
    loads[0].wait()
    loads[1].wait()
    loads[2].wait()
    got1[chip] = feat[pl.ds(pl.multiple_of(chip * PIECE, 16), PIECE), :]
    pl.semaphore_wait(barrier, len(plane) + NZ)

    send(owners_v, owners_mate_v, o_send, o_recv, yl_mate)
    near, across = lax.rem(yh + 2 * yl + NYH - 1, NYH), lax.rem(yh + 2, NYH)
    shares = [(2, across, 1 - yl), (1, across, 1 - yl), (3, across, 1 - yl), (0, across, 1 - yl)]
    shares += [(dx, near, yl_) for dx in (2, 1, 3, 0) for yl_ in range(NYL)]
    shares += [(dx, yh, yl) for dx in (2, 1, 3)]
    for dx, yh_, yl_ in shares:
        x_ = lax.rem(x + dx, NX)
        there = x_ * NYH + yh_
        send(
            feat.at[pl.ds(pl.multiple_of(there * PIECE, 16), PIECE), :],
            got1.at[chip], s_send.at[0], s1_recv, dev(x_, yh_, core, z, yl_),
        )

    for copy in loads[3:]:
        copy.wait()
    own = feat[pl.ds(pl.multiple_of(rep * SHARE, 16), SHARE), :]
    pre_own[...] = jnp.dot(own, w_self[...], preferred_element_type=F32) + bias[...]
    for s in range(SECTIONS):
        mask_copies[s].wait()

        def lower(k, carry, s=s):
            mask_low[s, k] = mask_raw[s, k].astype(F32).astype(BF16)
            return carry

        lax.fori_loop(0, SLOTS, lower, 0, unroll=2)

    def chain(t, ends):
        s = lax.rem(2 * core + t, SECTIONS)
        count = tcnt[0, 0, s]
        ends = list(ends)
        for k in range(SLOTS):
            live = jnp.minimum(jnp.maximum(count - k, 0), 1)
            spot = 1 + t * SLOTS + k
            link = 0
            for r in range(RT):
                gap = trow[0, 0, s, k] - r
                same = live * (1 - jnp.minimum(gap * gap, 1))
                link = link + same * ends[r]
                ends[r] = ends[r] + same * (spot - ends[r])
            before[t, k] = link
        return tuple(ends)

    ends = lax.fori_loop(0, SECTIONS, chain, (jnp.int32(0),) * RT)
    for r in range(RT):
        last[r] = ends[r]
    sums[0] = jnp.zeros((TILE, F_IN), F32)
    arrived(owners_mate_v, o_recv)
    fetch = pltpu.make_async_copy(owners_mate_v, owners_mate, o_copy)
    fetch.start()
    fetch.wait()
    arrived(got1.at[pl.ds(0, CHIPS - 1)], s1_recv)

    def chosen(table, s):
        owner = table[0, s]
        piece = jnp.zeros((PIECE, F_IN), F32)
        for b in range(CHIPS):
            gap = owner - (NC * b + core)
            piece = piece + got1[b].astype(F32) * (1 - jnp.minimum(gap * gap, 1)).astype(F32)
        return piece

    for t in range(2):
        give_core[0, t] = chosen(owners, 2 * other + t).astype(BF16)
        give_core[1, t] = chosen(owners_mate, 2 * other + t).astype(BF16)
    send(give_core, got_core, s_send.at[1], core_recv, core_mate)
    mine = [chosen(table, 2 * core + t) for table in (owners, owners_mate) for t in range(2)]
    arrived(got_core, core_recv)
    place = pl.ds(pl.multiple_of(chip * PIECE, 16), PIECE)
    for t in range(2):
        feats[2 * core + t, place, :] = (mine[t] + got_core[0, t].astype(F32)).astype(BF16)
        part_mate[t] = (mine[2 + t] + got_core[1, t].astype(F32)).astype(BF16)

    here = feats.at[pl.ds(2 * core, 2), place, :]

    def line(x_):
        start = pl.multiple_of(x_ * (NYH * PIECE), 16)
        return feats.at[pl.ds(2 * core, 2), pl.ds(start, NYH * PIECE), :]

    def part(x_, yh_):
        start = pl.multiple_of((x_ * NYH + yh_) * PIECE, 16)
        return feats.at[pl.ds(2 * core, 2), pl.ds(start, PIECE), :]

    right, left, far = lax.rem(x + 1, NX), lax.rem(x + 3, NX), lax.rem(x + 2, NX)
    to_right, to_left, to_far = (dev(x_, yh, core, z, yl) for x_ in (right, left, far))
    beside = lax.rem(yh + 1 - 2 * yl + NYH, NYH)
    send(part_mate, here, s_send.at[2], yrecv.at[2], dev(x, across, core, z, 1 - yl))
    send(part_mate, here, s_send.at[2], yrecv.at[0], dev(x, near, core, z, 1 - yl))
    send(here, here, s_send.at[2], yrecv.at[1], dev(x, near, core, z, yl))

    def sideways(n, yh_):
        for k, device in enumerate((to_far, to_right, to_left)):
            send(part(x, yh_), part(x, yh_), s_send.at[3], xrecv.at[k], device)

    sideways(0, yh)
    arrived(part(x, near), yrecv.at[0])
    sideways(1, near)
    arrived(part(x, beside), yrecv.at[1])
    sideways(2, beside)
    arrived(part(x, across), yrecv.at[2])
    sideways(3, across)
    send(line(x), line(x), half_send, half_recv.at[0], core_mate)
    for n, source in ((1, left), (2, right), (0, far)):
        arrived(line(source), xrecv.at[n])
        send(line(source), line(source), half_send, half_recv.at[n or 3], core_mate)

    def multiply(t):
        s = lax.rem(2 * core + t, SECTIONS)
        for c in range(RT):
            tiles[c] = feats[s, TILE * c:TILE * c + TILE, :]

        def one(k, carry):
            prods[k] = jnp.dot(mask_low[s, k], tiles[tcol[0, 0, s, k]], preferred_element_type=F32)
            return carry

        def link(k, carry):
            sums[1 + t * SLOTS + k] = prods[k] + sums[before[t, k]]
            return carry

        lax.fori_loop(0, SLOTS, one, 0, unroll=8)
        lax.fori_loop(0, SLOTS, link, 0)

    multiply(0)
    multiply(1)
    far_half = feats.at[pl.ds(2 * other, 2)]
    for n in range(4):
        arrived(far_half.at[:, pl.ds(0, NYH * PIECE), :], half_recv.at[n])
    multiply(2)
    multiply(3)

    order = [lax.rem(lax.div(z, 2) + step, RT) for step in (3, 2, 4, 1, 5, 0)]
    for r in order:
        acc[pl.ds(4 * r, 4)] = sums[last[r]].reshape(4, SHARE, F_IN)
        for h in range(2):
            y_out[2 * r + h] = acc[4 * r + 2 * h + 1 - yl].astype(BF16)
        send(y_out.at[pl.ds(2 * r, 2)], y_in.at[pl.ds(2 * r, 2)], yl_send, yl_recv.at[r], yl_mate)

    for step, r in enumerate(order):
        arrived(y_in.at[pl.ds(2 * r, 2)], yl_recv.at[r])
        for h in range(2):
            z_ = 2 * r + h
            both = acc[4 * r + 2 * h + yl] + y_in[z_].astype(F32)
            acc[4 * r + 2 * h + yl] = both
            z_out[z_] = both.astype(BF16)
            if step < RT - 1:
                send(z_out.at[z_], z_in.at[z], z_send, z_recv, dev(x, yh, core, z_, yl))
            else:
                @pl.when(z_ != z)
                def _(z_=z_):
                    send(z_out.at[z_], z_in.at[z], z_send, z_recv, dev(x, yh, core, z_, yl))

    z_in[z] = jnp.zeros((SHARE, F_IN), BF16)
    lanes = lax.broadcasted_iota(jnp.int32, (SHARE, SHARE), 1)
    subs = lax.broadcasted_iota(jnp.int32, (SHARE, SHARE), 0)
    deg = jnp.sum(jnp.where(lanes == subs, degree[...].astype(F32), 0.0), axis=1, keepdims=True)
    total = acc[2 * z + yl]
    arrived(z_in.at[pl.ds(0, NZ - 1)], z_recv)
    for z_ in range(NZ):
        total = total + z_in[z_].astype(F32)

    mean = (total / deg).astype(BF16)
    pre = pre_own[...] + jnp.dot(mean, w_neigh[...], preferred_element_type=F32)
    fall = jnp.exp(jnp.minimum(pre, 0.0))
    up = pre > 0
    hidden[...] = jnp.where(up, pre, fall - 1.0).astype(BF16)
    grad_pre = cot[...].astype(F32) * jnp.where(up, 1.0, fall)
    grad_low = grad_pre.astype(BF16)
    part_bias = jnp.sum(grad_pre, axis=0, keepdims=True)
    first_core = core == 0
    pair_out[:, 0:F_IN] = jnp.where(first_core, mean, own)
    pair_out[:, F_IN:] = grad_low
    bias_out[...] = jnp.broadcast_to(
        jnp.where(first_core, part_bias[:, F_IN:], part_bias[:, :F_IN]), (8, F_IN)
    )
    send(pair_out, pair_in, g_send.at[0], g_recv.at[0], core_mate)
    send(bias_out, bias_in, g_send.at[1], g_recv.at[1], core_mate)
    over_nodes = (((0,), (0,)), ((), ()))
    part = lax.dot_general(jnp.where(first_core, own, mean), grad_low, over_nodes, preferred_element_type=F32)
    half_bias = jnp.where(first_core, part_bias[:, :F_IN], part_bias[:, F_IN:])
    arrived(pair_in, g_recv.at[0])
    arrived(bias_in, g_recv.at[1])
    part = part + lax.dot_general(
        pair_in[:, 0:F_IN], pair_in[:, F_IN:], over_nodes, preferred_element_type=F32
    )
    bias_tile[...] = half_bias + bias_in[...]
    for o in range(OWNERS):
        m1[o] = part[16 * (o // 2):16 * (o // 2) + 16, TILE * (o % 2):TILE * (o % 2) + TILE].astype(BF16)
    pair_y = lax.div(y, 2)
    me_o = x * (NY // 2) + pair_y
    is_owner = lax.rem(y, 2) == core
    no_owner = lax.rem(y, 2) != core
    is_home = me_q == other
    no_home = me_q != other
    home = at_plane(0, other)
    for dx in (2, 1, 3, 0):
        for k in (2, 1, 3, 0):
            x_, h_ = lax.rem(x + dx, NX), lax.rem(pair_y + k, NY // 2)
            o_, device = x_ * (NY // 2) + h_, at_plane(x_, 2 * h_ + core)
            if dx or k:
                send(m1.at[o_], r1.at[me_q], g_send.at[2], g_recv.at[2], device)
            else:
                @pl.when(no_owner)
                def _():
                    send(m1.at[o_], r1.at[me_q], g_send.at[2], g_recv.at[2], device)

    @pl.when(no_home)
    def _():
        send(bias_tile, rb.at[me_q], g_send.at[7], g_recv.at[7], home)

    far_z = (6, 5, 7, 4, 8, 3, 9, 2, 10, 1, 11)
    norm = float(NODES) ** -0.5

    @pl.when(is_owner)
    def _():
        r1[me_q] = m1[me_o]
        arrived(r1.at[pl.ds(0, NX * NY - 1)], g_recv.at[2])
        level = r1[0].astype(F32)
        for q in range(1, NX * NY):
            level = level + r1[q].astype(F32)
        m3[...] = level.astype(BF16)
        for dz in far_z:
            send(m3, r3.at[z], g_send.at[3], g_recv.at[3], dev(x, yh, core, lax.rem(z + dz, NZ), yl))
        r3[z] = m3[...]
        arrived(r3.at[pl.ds(0, NZ - 1)], g_recv.at[3])
        level = r3[0].astype(F32)
        for k in range(1, NZ):
            level = level + r3[k].astype(F32)
        m4[...] = (level * norm).astype(BF16)
        for x_, y_ in plane:
            send(m4, r4.at[me_o], g_send.at[4], g_recv.at[4], at_plane(x_, y_))
        r4[me_o] = m4[...]
        arrived(r4.at[pl.ds(0, OWNERS - 1)], g_recv.at[4])

    @pl.when(is_home)
    def _():
        rb[me_q] = bias_tile[...]
        arrived(rb.at[pl.ds(0, NX * NY - 1)], g_recv.at[7])
        level = rb[0]
        for q in range(1, NX * NY):
            level = level + rb[q]
        m3b[...] = level
        for dz in far_z:
            send(m3b, r3b.at[z], g_send.at[8], g_recv.at[8], dev(x, yh, core, lax.rem(z + dz, NZ), yl))
        r3b[z] = level
        arrived(r3b.at[pl.ds(0, NZ - 1)], g_recv.at[8])
        level = r3b[0]
        for k in range(1, NZ):
            level = level + r3b[k]
        bias_sum[...] = level * norm
        for x_, y_ in plane:
            send(bias_sum, bias_sum, g_send.at[9], g_recv.at[9], at_plane(x_, y_))

    @pl.when(no_home)
    def _():
        arrived(bias_sum, g_recv.at[9])

    send(bias_sum, bias_far, g_send.at[6], g_recv.at[6], core_mate)

    @pl.when(no_owner)
    def _():
        arrived(r4, g_recv.at[4])

    send(r4, r5, g_send.at[5], g_recv.at[5], core_mate)
    grads[core] = r4[...]

    arrived(owners_v, o_send)
    arrived(got1.at[pl.ds(0, CHIPS - 1)], s_send.at[0])
    arrived(give_core, s_send.at[1])
    arrived(feats.at[0, pl.ds(0, 6 * PIECE), :], s_send.at[2])
    arrived(feats.at[pl.ds(0, 3), pl.ds(0, 8 * PIECE), :], s_send.at[3])
    arrived(feats.at[pl.ds(0, 2)], half_send)
    arrived(y_out, yl_send)
    arrived(z_out.at[pl.ds(0, NZ - 1)], z_send)
    arrived(pair_out, g_send.at[0])
    arrived(bias_out, g_send.at[1])
    @pl.when(is_owner)
    def _():
        arrived(m1.at[pl.ds(0, OWNERS - 1)], g_send.at[2])
        arrived(r3.at[pl.ds(0, NZ - 1)], g_send.at[3])
        arrived(r1.at[pl.ds(0, NX * NY - 1)], g_send.at[4])

    @pl.when(no_owner)
    def _():
        arrived(m1, g_send.at[2])

    @pl.when(is_home)
    def _():
        arrived(r3b.at[pl.ds(0, NZ - 1)], g_send.at[8])
        arrived(rb.at[pl.ds(0, NX * NY - 1)], g_send.at[9])

    @pl.when(no_home)
    def _():
        arrived(bias_tile, g_send.at[7])

    arrived(bias_sum, g_send.at[6])
    arrived(r4, g_send.at[5])

    arrived(bias_far, g_recv.at[6])
    near_bias, far_bias = bias_sum[0:1, :], bias_far[0:1, :]
    g_bias[:, 0:F_IN] = jnp.where(first_core, near_bias, far_bias)
    g_bias[:, F_IN:] = jnp.where(first_core, far_bias, near_bias)
    arrived(r5, g_recv.at[5])
    grads[other] = r5[...]


def spread(hidden_in, grads_h, bias_in, hidden, g_self, g_neigh, g_bias, grads_in, sems):
    moves = [
        pltpu.make_async_copy(a, b, sems.at[n])
        for n, (a, b) in enumerate(((grads_h, grads_in), (hidden_in, hidden), (bias_in, g_bias)))
    ]
    for move in moves:
        move.start()
    moves[0].wait()
    for half, target in enumerate((g_self, g_neigh)):
        for o in range(OWNERS):
            target[16 * (o // 2):16 * (o // 2) + 16, TILE * (o % 2):TILE * (o % 2) + TILE] = grads_in[
                half, o
            ].astype(F32)
    moves[1].wait()
    moves[2].wait()


def body(
    features, self_weight, neigh_weight, bias, degree, cotangent, owners, tile_rows, tile_cols, tile_count, masks
):
    vmem = pl.BlockSpec(memory_space=pltpu.VMEM)
    dma = pltpu.SemaphoreType.DMA
    hidden, grads, g_bias = pl.pallas_call(
        kernel,
        out_shape=(
            jax.ShapeDtypeStruct((SHARE, F), BF16),
            jax.ShapeDtypeStruct((NC, OWNERS, 16, TILE), BF16),
            jax.ShapeDtypeStruct((1, F), F32),
        ),
        in_specs=[pl.BlockSpec(memory_space=pl.ANY)] * 11,
        out_specs=(vmem,) * 3,
        scratch_shapes=[
            pltpu.VMEM((ROWS, F_IN), BF16),
            pltpu.VMEM((F_IN, F), BF16),
            pltpu.VMEM((F_IN, F), BF16),
            pltpu.VMEM((1, F), F32),
            pltpu.VMEM((1, SHARE), jnp.int32),
            pltpu.VMEM((SHARE, F), BF16),
            pltpu.SMEM((1, SECTIONS), jnp.int32),
            pltpu.VMEM((1, SECTIONS), jnp.int32),
            pltpu.VMEM((1, SECTIONS), jnp.int32),
            pltpu.SMEM((1, SECTIONS), jnp.int32),
            pltpu.SMEM((1, 1, SECTIONS, SLOTS), jnp.int32),
            pltpu.SMEM((1, 1, SECTIONS, SLOTS), jnp.int32),
            pltpu.SMEM((1, 1, SECTIONS), jnp.int32),
            pltpu.SMEM((SECTIONS, SLOTS), jnp.int32),
            pltpu.SMEM((RT,), jnp.int32),
            pltpu.VMEM((SECTIONS, SLOTS, TILE, TILE), jnp.int32),
            pltpu.VMEM((SECTIONS, SLOTS, TILE, TILE), BF16),
            pltpu.VMEM((CHIPS, PIECE, F_IN), BF16),
            pltpu.VMEM((2, 2, PIECE, F_IN), BF16),
            pltpu.VMEM((2, 2, PIECE, F_IN), BF16),
            pltpu.VMEM((SECTIONS, ROWS, F_IN), BF16),
            pltpu.VMEM((2, PIECE, F_IN), BF16),
            pltpu.VMEM((RT, TILE, F_IN), BF16),
            pltpu.VMEM((SLOTS, TILE, F_IN), F32),
            pltpu.VMEM((1 + SECTIONS * SLOTS, TILE, F_IN), F32),
            pltpu.VMEM((NZ * NYL, SHARE, F_IN), F32),
            pltpu.VMEM((NZ, SHARE, F_IN), BF16),
            pltpu.VMEM((NZ, SHARE, F_IN), BF16),
            pltpu.VMEM((NZ, SHARE, F_IN), BF16),
            pltpu.VMEM((NZ, SHARE, F_IN), BF16),
            pltpu.VMEM((SHARE, F), F32),
            pltpu.VMEM((SHARE, F_IN + F), BF16),
            pltpu.VMEM((SHARE, F_IN + F), BF16),
            pltpu.VMEM((8, F_IN), F32),
            pltpu.VMEM((8, F_IN), F32),
            pltpu.VMEM((8, F_IN), F32),
            pltpu.VMEM((8, F_IN), F32),
            pltpu.VMEM((OWNERS, 16, TILE), BF16),
            pltpu.VMEM((NX * NY, 16, TILE), BF16),
            pltpu.VMEM((16, TILE), BF16),
            pltpu.VMEM((NZ, 16, TILE), BF16),
            pltpu.VMEM((16, TILE), BF16),
            pltpu.VMEM((OWNERS, 16, TILE), BF16),
            pltpu.VMEM((OWNERS, 16, TILE), BF16),
            pltpu.VMEM((8, TILE), F32),
            pltpu.VMEM((NX * NY, 8, TILE), F32),
            pltpu.VMEM((8, TILE), F32),
            pltpu.VMEM((NZ, 8, TILE), F32),
            dma((11,)),
            dma((SECTIONS,)),
            dma,
            dma,
            dma,
            dma((4,)),
            dma,
            dma,
            dma((3,)),
            dma((3,)),
            dma,
            dma((4,)),
            dma,
            dma((RT,)),
            dma,
            dma,
            dma((10,)),
            dma((10,)),
        ],
        compiler_params=pltpu.CompilerParams(
            collective_id=0, has_side_effects=True, vmem_limit_bytes=60 * 1024 * 1024
        ),
    )(
        features, self_weight, neigh_weight, bias.reshape(1, F), degree.reshape(1, SHARE), cotangent,
        owners, tile_rows, tile_cols, tile_count, masks.reshape(SECTIONS, SLOTS, TILE, TILE),
    )
    hidden, g_self, g_neigh, g_bias = pl.pallas_call(
        spread,
        out_shape=(
            jax.ShapeDtypeStruct((SHARE, F), BF16),
            jax.ShapeDtypeStruct((F_IN, F), F32),
            jax.ShapeDtypeStruct((F_IN, F), F32),
            jax.ShapeDtypeStruct((1, F), F32),
        ),
        in_specs=[pl.BlockSpec(memory_space=pl.ANY)] * 3,
        out_specs=(
            pl.BlockSpec(memory_space=pl.ANY), vmem, vmem, pl.BlockSpec(memory_space=pl.ANY)
        ),
        scratch_shapes=[pltpu.VMEM((NC, OWNERS, 16, TILE), BF16), pltpu.SemaphoreType.DMA((3,))],
        compiler_params=pltpu.CompilerParams(vmem_limit_bytes=60 * 1024 * 1024),
    )(hidden, grads, g_bias)
    return hidden, g_self, g_neigh, g_bias.reshape(F)


def solution(mesh):
    return jax.shard_map(
        body,
        mesh=mesh,
        in_specs=(
            P("rows", None),
            P(),
            P(),
            P(),
            P(("rows", "rep")),
            P(("rows", "rep"), None),
            P("rep", None),
            P("rows", "rep", None, None),
            P("rows", "rep", None, None),
            P("rows", "rep", None),
            P("rows", "rep", None, None, None, None),
        ),
        out_specs=(P(("rows", "rep"), None), P(), P(), P()),
        check_vma=False,
    )
```

```python
import functools

import jax
import jax.numpy as jnp
from jax import lax
from jax.experimental import pallas as pl
from jax.experimental.pallas import tpu as pltpu
from jax.sharding import PartitionSpec as P

MESH = pl.DeviceIdType.MESH
NX, NYH, NC, NZ, NYL = 4, 4, 2, 12, 2
NY = NYH * NYL
TILE = 128
RT = 6
SECTIONS = 4
SLOTS = 16
ROWS = 768
CHIPS = NX * NYH
PIECE = ROWS // CHIPS
SHARE = ROWS // (NZ * NYL)
OWNERS = NX * NY // 2
F_IN = 128
F = 256
NODES = 24576
F32 = jnp.float32
BF16 = jnp.bfloat16


def kernel(
    feat_h, w_self_h, w_neigh_h, bias_h, degree_h, cot_h, owners_h, trow_h, tcol_h, tcnt_h, masks,
    hidden, grads, g_bias,
    feat, w_self, w_neigh, bias, degree, cot, owners, owners_v, owners_mate_v, owners_mate, trow, tcol, tcnt,
    before, last, mask_raw, mask_low, got1, give_core, got_core, feats, part_mate, tiles, prods, sums, acc, y_out, y_in,
    z_out, z_in, pre_own, pair_out, pair_in, bias_out, bias_in, bias_sum, bias_far,
    m1, r1, m3, r3, m4, r4, r5, bias_tile, rb, m3b, r3b,
    in_sem, mask_sem, o_send, o_recv, o_copy, s_send, s1_recv, core_recv, yrecv, xrecv, half_send, half_recv,
    yl_send, yl_recv, z_send, z_recv, g_send, g_recv,
):
    row, rep = lax.axis_index("rows"), lax.axis_index("rep")
    core = lax.rem(row, NC)
    chip = lax.div(row, NC)
    yh = lax.rem(chip, NYH)
    x = lax.div(chip, NYH)
    yl = lax.rem(rep, NYL)
    z = lax.div(rep, NYL)
    y = yh * NYL + yl
    other = 1 - core

    def dev(x_, yh_, c_, z_, yl_):
        return ((x_ * NYH + yh_) * NC + c_, z_ * NYL + yl_)

    def at_plane(x_, y_):
        return dev(x_, lax.div(y_, NYL), core, z, lax.rem(y_, NYL))

    def send(src, dst, ssem, rsem, device):
        copy = pltpu.make_async_remote_copy(
            src_ref=src, dst_ref=dst, send_sem=ssem, recv_sem=rsem, device_id=device, device_id_type=MESH
        )
        copy.start()

    def arrived(buf, sem):
        pltpu.make_async_copy(buf, buf, sem).wait()

    core_mate = dev(x, yh, other, z, yl)
    yl_mate = dev(x, yh, core, z, 1 - yl)
    plane = [(lax.rem(x + dx, NX), lax.rem(y + dy, NY)) for dx in (2, 1, 3, 0) for dy in (4, 3, 5, 2, 6, 1, 7, 0)]
    plane = plane[:-1]
    me_q = x * NY + y

    pairs = (
        (feat_h, feat), (owners_h, owners_v), (owners_h, owners), (w_self_h, w_self), (bias_h, bias), (trow_h, trow), (tcol_h, tcol),
        (tcnt_h, tcnt), (w_neigh_h, w_neigh), (degree_h, degree), (cot_h, cot),
    )
    loads = [pltpu.make_async_copy(a, b, in_sem.at[n]) for n, (a, b) in enumerate(pairs)]
    loads[0].start()
    barrier = pltpu.get_barrier_semaphore()

    def greet(device):
        pl.semaphore_signal(barrier, inc=1, device_id=device, device_id_type=MESH)

    for dz in (6, 5, 7, 4, 8, 3, 9, 2, 10, 1, 11):
        greet(dev(x, yh, core, lax.rem(z + dz, NZ), yl))
    for x_, y_ in plane:
        greet(at_plane(x_, y_))
    greet(core_mate)

    for copy in loads[1:]:
        copy.start()
    mask_copies = [
        pltpu.make_async_copy(masks.at[s], mask_raw.at[s], mask_sem.at[s]) for s in range(SECTIONS)
    ]
    for copy in mask_copies:
        copy.start()
    pl.semaphore_wait(barrier, len(plane) + NZ)

    near, across = lax.rem(yh + 2 * yl + NYH - 1, NYH), lax.rem(yh + 2, NYH)
    shares = [(2, across, 1 - yl), (1, across, 1 - yl), (3, across, 1 - yl), (0, across, 1 - yl)]
    shares += [(dx, near, yl_) for dx in (2, 1, 3, 0) for yl_ in range(NYL)]
    shares += [(dx, yh, yl) for dx in (2, 1, 3)]
    for dx, yh_, yl_ in shares:
        x_ = lax.rem(x + dx, NX)
        there = x_ * NYH + yh_
        send(
            feat_h.at[pl.ds(pl.multiple_of(there * PIECE, 16), PIECE), :],
            got1.at[chip], s_send.at[0], s1_recv, dev(x_, yh_, core, z, yl_),
        )

    loads[1].wait()
    send(owners_v, owners_mate_v, o_send, o_recv, yl_mate)
    loads[0].wait()
    got1[chip] = feat[pl.ds(pl.multiple_of(chip * PIECE, 16), PIECE), :]
    for copy in loads[2:]:
        copy.wait()
    own = feat[pl.ds(pl.multiple_of(rep * SHARE, 16), SHARE), :]
    pre_own[...] = jnp.dot(own, w_self[...], preferred_element_type=F32) + bias[...]
    for s in range(SECTIONS):
        mask_copies[s].wait()

        def lower(k, carry, s=s):
            mask_low[s, k] = mask_raw[s, k].astype(F32).astype(BF16)
            return carry

        lax.fori_loop(0, SLOTS, lower, 0, unroll=2)

    def chain(t, ends):
        s = lax.rem(2 * core + t, SECTIONS)
        count = tcnt[0, 0, s]
        ends = list(ends)
        for k in range(SLOTS):
            live = jnp.minimum(jnp.maximum(count - k, 0), 1)
            spot = 1 + t * SLOTS + k
            link = 0
            for r in range(RT):
                gap = trow[0, 0, s, k] - r
                same = live * (1 - jnp.minimum(gap * gap, 1))
                link = link + same * ends[r]
                ends[r] = ends[r] + same * (spot - ends[r])
            before[t, k] = link
        return tuple(ends)

    ends = lax.fori_loop(0, SECTIONS, chain, (jnp.int32(0),) * RT)
    for r in range(RT):
        last[r] = ends[r]
    sums[0] = jnp.zeros((TILE, F_IN), F32)
    arrived(owners_mate_v, o_recv)
    fetch = pltpu.make_async_copy(owners_mate_v, owners_mate, o_copy)
    fetch.start()
    fetch.wait()
    arrived(got1.at[pl.ds(0, CHIPS - 1)], s1_recv)

    def chosen(table, s):
        owner = table[0, s]
        piece = jnp.zeros((PIECE, F_IN), F32)
        for b in range(CHIPS):
            gap = owner - (NC * b + core)
            piece = piece + got1[b].astype(F32) * (1 - jnp.minimum(gap * gap, 1)).astype(F32)
        return piece

    for t in range(2):
        give_core[0, t] = chosen(owners, 2 * other + t).astype(BF16)
        give_core[1, t] = chosen(owners_mate, 2 * other + t).astype(BF16)
    send(give_core, got_core, s_send.at[1], core_recv, core_mate)
    mine = [chosen(table, 2 * core + t) for table in (owners, owners_mate) for t in range(2)]
    arrived(got_core, core_recv)
    place = pl.ds(pl.multiple_of(chip * PIECE, 16), PIECE)
    for t in range(2):
        feats[2 * core + t, place, :] = (mine[t] + got_core[0, t].astype(F32)).astype(BF16)
        part_mate[t] = (mine[2 + t] + got_core[1, t].astype(F32)).astype(BF16)

    here = feats.at[pl.ds(2 * core, 2), place, :]

    def line(x_):
        start = pl.multiple_of(x_ * (NYH * PIECE), 16)
        return feats.at[pl.ds(2 * core, 2), pl.ds(start, NYH * PIECE), :]

    def part(x_, yh_):
        start = pl.multiple_of((x_ * NYH + yh_) * PIECE, 16)
        return feats.at[pl.ds(2 * core, 2), pl.ds(start, PIECE), :]

    right, left, far = lax.rem(x + 1, NX), lax.rem(x + 3, NX), lax.rem(x + 2, NX)
    to_right, to_left, to_far = (dev(x_, yh, core, z, yl) for x_ in (right, left, far))
    beside = lax.rem(yh + 1 - 2 * yl + NYH, NYH)
    send(part_mate, here, s_send.at[2], yrecv.at[2], dev(x, across, core, z, 1 - yl))
    send(part_mate, here, s_send.at[2], yrecv.at[0], dev(x, near, core, z, 1 - yl))
    send(here, here, s_send.at[2], yrecv.at[1], dev(x, near, core, z, yl))

    def sideways(n, yh_):
        for k, device in enumerate((to_far, to_right, to_left)):
            send(part(x, yh_), part(x, yh_), s_send.at[3], xrecv.at[k], device)

    sideways(0, yh)
    arrived(part(x, near), yrecv.at[0])
    sideways(1, near)
    arrived(part(x, beside), yrecv.at[1])
    sideways(2, beside)
    arrived(part(x, across), yrecv.at[2])
    sideways(3, across)
    send(line(x), line(x), half_send, half_recv.at[0], core_mate)
    for n, source in ((1, left), (2, right), (0, far)):
        arrived(line(source), xrecv.at[n])
        send(line(source), line(source), half_send, half_recv.at[n or 3], core_mate)

    def multiply(t):
        s = lax.rem(2 * core + t, SECTIONS)
        for c in range(RT):
            tiles[c] = feats[s, TILE * c:TILE * c + TILE, :]

        def one(k, carry):
            prods[k] = jnp.dot(mask_low[s, k], tiles[tcol[0, 0, s, k]], preferred_element_type=F32)
            return carry

        def link(k, carry):
            sums[1 + t * SLOTS + k] = prods[k] + sums[before[t, k]]
            return carry

        lax.fori_loop(0, SLOTS, one, 0, unroll=8)
        lax.fori_loop(0, SLOTS, link, 0)

    multiply(0)
    multiply(1)
    far_half = feats.at[pl.ds(2 * other, 2)]
    for n in range(4):
        arrived(far_half.at[:, pl.ds(0, NYH * PIECE), :], half_recv.at[n])
    multiply(2)
    multiply(3)

    order = [lax.rem(lax.div(z, 2) + step, RT) for step in (3, 2, 4, 1, 5, 0)]
    for r in order:
        acc[pl.ds(4 * r, 4)] = sums[last[r]].reshape(4, SHARE, F_IN)
        for h in range(2):
            y_out[2 * r + h] = acc[4 * r + 2 * h + 1 - yl].astype(BF16)
        send(y_out.at[pl.ds(2 * r, 2)], y_in.at[pl.ds(2 * r, 2)], yl_send, yl_recv.at[r], yl_mate)

    for step, r in enumerate(order):
        arrived(y_in.at[pl.ds(2 * r, 2)], yl_recv.at[r])
        for h in range(2):
            z_ = 2 * r + h
            both = acc[4 * r + 2 * h + yl] + y_in[z_].astype(F32)
            acc[4 * r + 2 * h + yl] = both
            z_out[z_] = both.astype(BF16)
            if step < RT - 1:
                send(z_out.at[z_], z_in.at[z], z_send, z_recv, dev(x, yh, core, z_, yl))
            else:
                @pl.when(z_ != z)
                def _(z_=z_):
                    send(z_out.at[z_], z_in.at[z], z_send, z_recv, dev(x, yh, core, z_, yl))

    z_in[z] = jnp.zeros((SHARE, F_IN), BF16)
    lanes = lax.broadcasted_iota(jnp.int32, (SHARE, SHARE), 1)
    subs = lax.broadcasted_iota(jnp.int32, (SHARE, SHARE), 0)
    deg = jnp.sum(jnp.where(lanes == subs, degree[...].astype(F32), 0.0), axis=1, keepdims=True)
    total = acc[2 * z + yl]
    arrived(z_in.at[pl.ds(0, NZ - 1)], z_recv)
    for z_ in range(NZ):
        total = total + z_in[z_].astype(F32)

    mean = (total / deg).astype(BF16)
    pre = pre_own[...] + jnp.dot(mean, w_neigh[...], preferred_element_type=F32)
    fall = jnp.exp(jnp.minimum(pre, 0.0))
    up = pre > 0
    hidden[...] = jnp.where(up, pre, fall - 1.0).astype(BF16)
    grad_pre = cot[...].astype(F32) * jnp.where(up, 1.0, fall)
    grad_low = grad_pre.astype(BF16)
    part_bias = jnp.sum(grad_pre, axis=0, keepdims=True)
    first_core = core == 0
    pair_out[:, 0:F_IN] = jnp.where(first_core, mean, own)
    pair_out[:, F_IN:] = grad_low
    bias_out[...] = jnp.broadcast_to(
        jnp.where(first_core, part_bias[:, F_IN:], part_bias[:, :F_IN]), (8, F_IN)
    )
    send(pair_out, pair_in, g_send.at[0], g_recv.at[0], core_mate)
    send(bias_out, bias_in, g_send.at[1], g_recv.at[1], core_mate)
    over_nodes = (((0,), (0,)), ((), ()))
    part = lax.dot_general(jnp.where(first_core, own, mean), grad_low, over_nodes, preferred_element_type=F32)
    half_bias = jnp.where(first_core, part_bias[:, :F_IN], part_bias[:, F_IN:])
    arrived(pair_in, g_recv.at[0])
    arrived(bias_in, g_recv.at[1])
    part = part + lax.dot_general(
        pair_in[:, 0:F_IN], pair_in[:, F_IN:], over_nodes, preferred_element_type=F32
    )
    bias_tile[...] = half_bias + bias_in[...]
    for o in range(OWNERS):
        m1[o] = part[16 * (o // 2):16 * (o // 2) + 16, TILE * (o % 2):TILE * (o % 2) + TILE].astype(BF16)
    pair_y = lax.div(y, 2)
    me_o = x * (NY // 2) + pair_y
    is_owner = lax.rem(y, 2) == core
    no_owner = lax.rem(y, 2) != core
    is_home = me_q == other
    no_home = me_q != other
    home = at_plane(0, other)
    for dx in (2, 1, 3, 0):
        for k in (2, 1, 3, 0):
            x_, h_ = lax.rem(x + dx, NX), lax.rem(pair_y + k, NY // 2)
            o_, device = x_ * (NY // 2) + h_, at_plane(x_, 2 * h_ + core)
            if dx or k:
                send(m1.at[o_], r1.at[me_q], g_send.at[2], g_recv.at[2], device)
            else:
                @pl.when(no_owner)
                def _():
                    send(m1.at[o_], r1.at[me_q], g_send.at[2], g_recv.at[2], device)

    @pl.when(no_home)
    def _():
        send(bias_tile, rb.at[me_q], g_send.at[7], g_recv.at[7], home)

    far_z = (6, 5, 7, 4, 8, 3, 9, 2, 10, 1, 11)
    norm = float(NODES) ** -0.5

    @pl.when(is_owner)
    def _():
        r1[me_q] = m1[me_o]
        arrived(r1.at[pl.ds(0, NX * NY - 1)], g_recv.at[2])
        level = r1[0].astype(F32)
        for q in range(1, NX * NY):
            level = level + r1[q].astype(F32)
        m3[...] = level.astype(BF16)
        for dz in far_z:
            send(m3, r3.at[z], g_send.at[3], g_recv.at[3], dev(x, yh, core, lax.rem(z + dz, NZ), yl))
        r3[z] = m3[...]
        arrived(r3.at[pl.ds(0, NZ - 1)], g_recv.at[3])
        level = r3[0].astype(F32)
        for k in range(1, NZ):
            level = level + r3[k].astype(F32)
        m4[...] = (level * norm).astype(BF16)
        for x_, y_ in plane:
            send(m4, r4.at[me_o], g_send.at[4], g_recv.at[4], at_plane(x_, y_))
        r4[me_o] = m4[...]
        arrived(r4.at[pl.ds(0, OWNERS - 1)], g_recv.at[4])

    @pl.when(is_home)
    def _():
        rb[me_q] = bias_tile[...]
        arrived(rb.at[pl.ds(0, NX * NY - 1)], g_recv.at[7])
        level = rb[0]
        for q in range(1, NX * NY):
            level = level + rb[q]
        m3b[...] = level
        for dz in far_z:
            send(m3b, r3b.at[z], g_send.at[8], g_recv.at[8], dev(x, yh, core, lax.rem(z + dz, NZ), yl))
        r3b[z] = level
        arrived(r3b.at[pl.ds(0, NZ - 1)], g_recv.at[8])
        level = r3b[0]
        for k in range(1, NZ):
            level = level + r3b[k]
        bias_sum[...] = level * norm
        for x_, y_ in plane:
            send(bias_sum, bias_sum, g_send.at[9], g_recv.at[9], at_plane(x_, y_))

    @pl.when(no_home)
    def _():
        arrived(bias_sum, g_recv.at[9])

    send(bias_sum, bias_far, g_send.at[6], g_recv.at[6], core_mate)

    @pl.when(no_owner)
    def _():
        arrived(r4, g_recv.at[4])

    send(r4, r5, g_send.at[5], g_recv.at[5], core_mate)
    grads[core] = r4[...]

    arrived(owners_v, o_send)
    arrived(got1.at[pl.ds(0, CHIPS - 1)], s_send.at[0])
    arrived(give_core, s_send.at[1])
    arrived(feats.at[0, pl.ds(0, 6 * PIECE), :], s_send.at[2])
    arrived(feats.at[pl.ds(0, 3), pl.ds(0, 8 * PIECE), :], s_send.at[3])
    arrived(feats.at[pl.ds(0, 2)], half_send)
    arrived(y_out, yl_send)
    arrived(z_out.at[pl.ds(0, NZ - 1)], z_send)
    arrived(pair_out, g_send.at[0])
    arrived(bias_out, g_send.at[1])
    @pl.when(is_owner)
    def _():
        arrived(m1.at[pl.ds(0, OWNERS - 1)], g_send.at[2])
        arrived(r3.at[pl.ds(0, NZ - 1)], g_send.at[3])
        arrived(r1.at[pl.ds(0, NX * NY - 1)], g_send.at[4])

    @pl.when(no_owner)
    def _():
        arrived(m1, g_send.at[2])

    @pl.when(is_home)
    def _():
        arrived(r3b.at[pl.ds(0, NZ - 1)], g_send.at[8])
        arrived(rb.at[pl.ds(0, NX * NY - 1)], g_send.at[9])

    @pl.when(no_home)
    def _():
        arrived(bias_tile, g_send.at[7])

    arrived(bias_sum, g_send.at[6])
    arrived(r4, g_send.at[5])

    arrived(bias_far, g_recv.at[6])
    near_bias, far_bias = bias_sum[0:1, :], bias_far[0:1, :]
    g_bias[:, 0:F_IN] = jnp.where(first_core, near_bias, far_bias)
    g_bias[:, F_IN:] = jnp.where(first_core, far_bias, near_bias)
    arrived(r5, g_recv.at[5])
    grads[other] = r5[...]


def spread(hidden_in, grads_h, bias_in, hidden, g_self, g_neigh, g_bias, grads_in, sems):
    moves = [
        pltpu.make_async_copy(a, b, sems.at[n])
        for n, (a, b) in enumerate(((grads_h, grads_in), (hidden_in, hidden), (bias_in, g_bias)))
    ]
    for move in moves:
        move.start()
    moves[0].wait()
    for half, target in enumerate((g_self, g_neigh)):
        for o in range(OWNERS):
            target[16 * (o // 2):16 * (o // 2) + 16, TILE * (o % 2):TILE * (o % 2) + TILE] = grads_in[
                half, o
            ].astype(F32)
    moves[1].wait()
    moves[2].wait()


def body(
    features, self_weight, neigh_weight, bias, degree, cotangent, owners, tile_rows, tile_cols, tile_count, masks
):
    vmem = pl.BlockSpec(memory_space=pltpu.VMEM)
    dma = pltpu.SemaphoreType.DMA
    hidden, grads, g_bias = pl.pallas_call(
        kernel,
        out_shape=(
            jax.ShapeDtypeStruct((SHARE, F), BF16),
            jax.ShapeDtypeStruct((NC, OWNERS, 16, TILE), BF16),
            jax.ShapeDtypeStruct((1, F), F32),
        ),
        in_specs=[pl.BlockSpec(memory_space=pl.ANY)] * 11,
        out_specs=(vmem,) * 3,
        scratch_shapes=[
            pltpu.VMEM((ROWS, F_IN), BF16),
            pltpu.VMEM((F_IN, F), BF16),
            pltpu.VMEM((F_IN, F), BF16),
            pltpu.VMEM((1, F), F32),
            pltpu.VMEM((1, SHARE), jnp.int32),
            pltpu.VMEM((SHARE, F), BF16),
            pltpu.SMEM((1, SECTIONS), jnp.int32),
            pltpu.VMEM((1, SECTIONS), jnp.int32),
            pltpu.VMEM((1, SECTIONS), jnp.int32),
            pltpu.SMEM((1, SECTIONS), jnp.int32),
            pltpu.SMEM((1, 1, SECTIONS, SLOTS), jnp.int32),
            pltpu.SMEM((1, 1, SECTIONS, SLOTS), jnp.int32),
            pltpu.SMEM((1, 1, SECTIONS), jnp.int32),
            pltpu.SMEM((SECTIONS, SLOTS), jnp.int32),
            pltpu.SMEM((RT,), jnp.int32),
            pltpu.VMEM((SECTIONS, SLOTS, TILE, TILE), jnp.int32),
            pltpu.VMEM((SECTIONS, SLOTS, TILE, TILE), BF16),
            pltpu.VMEM((CHIPS, PIECE, F_IN), BF16),
            pltpu.VMEM((2, 2, PIECE, F_IN), BF16),
            pltpu.VMEM((2, 2, PIECE, F_IN), BF16),
            pltpu.VMEM((SECTIONS, ROWS, F_IN), BF16),
            pltpu.VMEM((2, PIECE, F_IN), BF16),
            pltpu.VMEM((RT, TILE, F_IN), BF16),
            pltpu.VMEM((SLOTS, TILE, F_IN), F32),
            pltpu.VMEM((1 + SECTIONS * SLOTS, TILE, F_IN), F32),
            pltpu.VMEM((NZ * NYL, SHARE, F_IN), F32),
            pltpu.VMEM((NZ, SHARE, F_IN), BF16),
            pltpu.VMEM((NZ, SHARE, F_IN), BF16),
            pltpu.VMEM((NZ, SHARE, F_IN), BF16),
            pltpu.VMEM((NZ, SHARE, F_IN), BF16),
            pltpu.VMEM((SHARE, F), F32),
            pltpu.VMEM((SHARE, F_IN + F), BF16),
            pltpu.VMEM((SHARE, F_IN + F), BF16),
            pltpu.VMEM((8, F_IN), F32),
            pltpu.VMEM((8, F_IN), F32),
            pltpu.VMEM((8, F_IN), F32),
            pltpu.VMEM((8, F_IN), F32),
            pltpu.VMEM((OWNERS, 16, TILE), BF16),
            pltpu.VMEM((NX * NY, 16, TILE), BF16),
            pltpu.VMEM((16, TILE), BF16),
            pltpu.VMEM((NZ, 16, TILE), BF16),
            pltpu.VMEM((16, TILE), BF16),
            pltpu.VMEM((OWNERS, 16, TILE), BF16),
            pltpu.VMEM((OWNERS, 16, TILE), BF16),
            pltpu.VMEM((8, TILE), F32),
            pltpu.VMEM((NX * NY, 8, TILE), F32),
            pltpu.VMEM((8, TILE), F32),
            pltpu.VMEM((NZ, 8, TILE), F32),
            dma((11,)),
            dma((SECTIONS,)),
            dma,
            dma,
            dma,
            dma((4,)),
            dma,
            dma,
            dma((3,)),
            dma((3,)),
            dma,
            dma((4,)),
            dma,
            dma((RT,)),
            dma,
            dma,
            dma((10,)),
            dma((10,)),
        ],
        compiler_params=pltpu.CompilerParams(
            collective_id=0, has_side_effects=True, vmem_limit_bytes=60 * 1024 * 1024
        ),
    )(
        features, self_weight, neigh_weight, bias.reshape(1, F), degree.reshape(1, SHARE), cotangent,
        owners, tile_rows, tile_cols, tile_count, masks.reshape(SECTIONS, SLOTS, TILE, TILE),
    )
    hidden, g_self, g_neigh, g_bias = pl.pallas_call(
        spread,
        out_shape=(
            jax.ShapeDtypeStruct((SHARE, F), BF16),
            jax.ShapeDtypeStruct((F_IN, F), F32),
            jax.ShapeDtypeStruct((F_IN, F), F32),
            jax.ShapeDtypeStruct((1, F), F32),
        ),
        in_specs=[pl.BlockSpec(memory_space=pl.ANY)] * 3,
        out_specs=(
            pl.BlockSpec(memory_space=pl.ANY), vmem, vmem, pl.BlockSpec(memory_space=pl.ANY)
        ),
        scratch_shapes=[pltpu.VMEM((NC, OWNERS, 16, TILE), BF16), pltpu.SemaphoreType.DMA((3,))],
        compiler_params=pltpu.CompilerParams(vmem_limit_bytes=60 * 1024 * 1024),
    )(hidden, grads, g_bias)
    return hidden, g_self, g_neigh, g_bias.reshape(F)


def solution(mesh):
    return jax.shard_map(
        body,
        mesh=mesh,
        in_specs=(
            P("rows", None),
            P(),
            P(),
            P(),
            P(("rows", "rep")),
            P(("rows", "rep"), None),
            P("rep", None),
            P("rows", "rep", None, None),
            P("rows", "rep", None, None),
            P("rows", "rep", None),
            P("rows", "rep", None, None, None, None),
        ),
        out_specs=(P(("rows", "rep"), None), P(), P(), P()),
        check_vma=False,
    )
```
